128 devices in a mesh: row: 8 (over z, core), col: 16 (over x, y).
Axes of the slice: x: 4, y: 4, z: 4, core: 2. Of those that a mesh axis runs over, the one named last changes fastest.
Arguments:
- tile_values: bfloat16 [8, 16, 40, 512, 512], P('row', 'col')
- tile_rows: int32 [8, 16, 40], P('row', 'col'), may hold values from 0 to 31
- tile_cols: int32 [8, 16, 40], P('row', 'col'), may hold values from 0 to 15
- start_basis: bfloat16 [131072, 256], P(('row', 'col')), may hold values from -6 to 6
Outputs:
- new_basis: float32 [131072, 256], P(('row', 'col'))
- triangle: float32 [256, 256], replicated
The draws below stay inside these ranges and needn't reach their ends.
All inputs are finite; a program needn't handle non-finite values.
Results may differ from the reference program's by a relative error of at most 0.002.
Values may be sent and summed in bfloat16 or wider, within the bound.
No kernel may reach another device: no remote copies, remote signals or barrier semaphores. Data moves between devices by JAX's collectives and lax.ppermute only.
A program may use at most 192 MiB of HBM per device.

```python
import math
import jax
import jax.numpy as jnp
from jax import lax

ORDER = 131072
TB = 512
RANK = 256
TILES_DEV = 40
BLOCKS = 256
ROWBLK = 32
COLBLK = 16
N_ROW = 8
N_COL = 16


def draw_tile_values(key, part):
    key = jax.random.fold_in(key, 11)
    value_key = jax.random.fold_in(key, 1)
    shape = (N_ROW, N_COL, TILES_DEV, TB, TB)
    per_column = N_ROW * N_COL * TILES_DEV * TB / ORDER
    scale = 1.0 / math.sqrt(per_column * TB)
    level = (jnp.arange(N_ROW, dtype=jnp.float32)[:, None] * TB + jnp.arange(TB, dtype=jnp.float32)[None, :]) / (N_ROW * TB)
    rising = jnp.exp(level * math.log(3.0)).reshape(N_ROW, 1, 1, TB, 1)
    values = jax.random.normal(value_key, shape, jnp.float32)
    return (values * scale * rising).astype(jnp.bfloat16)


def touch_ends(values, stream_key, least, high):
    dims = values.shape
    index_at = [jax.random.randint(jax.random.fold_in(stream_key, axis), (), 0, dims[axis]) for axis in range(len(dims))]
    values = values.at[tuple(index_at)].set(least)
    longest = dims.index(max(dims))
    index_at[longest] = (index_at[longest] + 1) % dims[longest]
    return values.at[tuple(index_at)].set(high)


def block_scale(key, extent, shards, low, top_value):
    gain = 1.0
    for axis_at, parts in shards:
        heights = jax.random.uniform(jax.random.fold_in(jax.random.fold_in(key, 6), axis_at), (parts,), jnp.float32, low / len(shards), top_value / len(shards))
        gain = gain * jnp.repeat(jnp.exp(heights), extent[axis_at] // parts).reshape((-1,) + (1,) * (len(extent) - 1 - axis_at))
    return gain


def centred(own_key, shape, scale, limit, split=(), kind=jnp.bfloat16):
    array = scale * jax.random.normal(own_key, shape, jnp.float32)
    if split:
        array = array * block_scale(own_key, shape, split, -0.22, 0.18)
    return jnp.clip(array, -limit, limit).astype(kind)


def setup_inputs(seed: int = 0) -> dict:
    arg_keys = jax.random.split(jax.random.key(seed), 5)
    tile_values = draw_tile_values(jax.random.fold_in(arg_keys[4], 71), 0)
    tile_rows = touch_ends(jax.random.randint(arg_keys[1], (N_ROW, N_COL, TILES_DEV), 0, ROWBLK), jax.random.fold_in(arg_keys[1], 1), 0, ROWBLK - 1).astype(jnp.int32)
    tile_cols = touch_ends(jax.random.randint(arg_keys[2], (N_ROW, N_COL, TILES_DEV), 0, COLBLK), jax.random.fold_in(arg_keys[2], 1), 0, COLBLK - 1).astype(jnp.int32)
    start_basis = centred(arg_keys[3], (ORDER, RANK), 1.0, 6.0, ((0, 128),))
    return {"tile_values": tile_values, "tile_rows": tile_rows, "tile_cols": tile_cols, "start_basis": start_basis}


def reference(tile_values, tile_rows, tile_cols, start_basis):
    qblocks = start_basis.astype(jnp.float32).reshape(BLOCKS, TB, RANK)
    device_ids = jnp.arange(N_ROW * N_COL, dtype=jnp.int32)

    def first(acc, index):
        row_dev = index // N_COL
        col_dev = index % N_COL
        local_tiles = tile_values[row_dev, col_dev].astype(jnp.float32)
        grow = (row_dev * ROWBLK + tile_rows[row_dev, col_dev]).astype(jnp.int32)
        gcol = (col_dev * COLBLK + tile_cols[row_dev, col_dev]).astype(jnp.int32)
        product = jnp.einsum('ktn,ktr->knr', local_tiles, qblocks[grow])
        return (acc.at[gcol].add(product), None)
    wide, _ = lax.scan(first, jnp.zeros((BLOCKS, TB, RANK), jnp.float32), device_ids)
    wide_half = wide.astype(jnp.bfloat16).astype(jnp.float32)

    def second(acc, index):
        row_dev = index // N_COL
        col_dev = index % N_COL
        local_tiles = tile_values[row_dev, col_dev].astype(jnp.float32)
        grow = (row_dev * ROWBLK + tile_rows[row_dev, col_dev]).astype(jnp.int32)
        gcol = (col_dev * COLBLK + tile_cols[row_dev, col_dev]).astype(jnp.int32)
        product = jnp.einsum('kmn,knr->kmr', local_tiles, wide_half[gcol])
        return (acc.at[grow].add(product), None)
    image, _ = lax.scan(second, jnp.zeros((BLOCKS, TB, RANK), jnp.float32), device_ids)
    image = image.reshape(ORDER, RANK)
    gram_matrix = jnp.dot(image.T, image, precision=lax.Precision.HIGHEST) / ORDER
    lower_factor = jnp.linalg.cholesky(gram_matrix)
    new_basis = jax.scipy.linalg.solve_triangular(lower_factor, image.T, lower=True).T
    return (new_basis, lower_factor.T)
```

```python
import functools

import jax
import jax.numpy as jnp
from jax import lax
from jax.experimental import pallas as pl
from jax.experimental.pallas import tpu as pltpu
from jax.sharding import PartitionSpec as P

ORDER = 131072
TB = 512
CHUNKS = 1
STEP = 4
PAD = 16
TINY = 1e-30
LIMIT = 60 * 2**20
VMEM = pl.BlockSpec(memory_space=pltpu.VMEM)
ANY = pl.BlockSpec(memory_space=pl.ANY)
F32 = jnp.float32

HOPS = (1, 3, 2)


def permute(value, axis, hop):
    if axis in ("z", "core"):
        name, size = "row", 8
        place = (lambda i: (i + 2 * hop) % 8) if axis == "z" else (lambda i: i ^ 1)
    else:
        name, size = "col", 16
        if axis == "x":
            place = lambda i: (i + 4 * hop) % 16
        else:
            place = lambda i: i // 4 * 4 + (i + hop) % 4
    return lax.ppermute(value, name, [(i, place(i)) for i in range(size)])


def slot_to(distance):
    return jnp.where(distance >= 2, 5 - distance, distance)


def slot_from(distance):
    return slot_to((4 - distance) % 4)


def params(**kw):
    return pltpu.CompilerParams(vmem_limit_bytes=LIMIT, **kw)


def exponent(top):
    return jnp.ceil(jnp.log2(jnp.maximum(top, TINY)) + 0.01) - 15.0


def code(value):
    power = exponent(jnp.max(jnp.abs(value), axis=0, keepdims=True))
    return jnp.round(value * jnp.exp2(-power)).astype(jnp.int16), power


def store_coded(ref, blocks):
    powers = []
    for i, value in enumerate(blocks):
        m = value.shape[0]
        ref[i * m : (i + 1) * m, :], power = code(value)
        powers.append(power)
    fill = jnp.zeros((PAD - len(powers), powers[0].shape[1]), F32)
    ref[-PAD:, :] = jnp.concatenate(powers + [fill], axis=0).astype(jnp.int16)


def units(ref):
    return jnp.exp2(ref[-PAD:, :].astype(F32))


def first_product(rows, cols, tiles, pieces, m):
    count = tiles.shape[0]
    n = len(pieces)

    def body(row_ref, col_ref, tile_ref, *rest):
        ins, keep_ref, send_ref, basis, acc, sems = (
            rest[:n],
            rest[n],
            rest[n + 1],
            rest[n + 2],
            rest[n + 3],
            rest[n + 4],
        )
        step = pl.program_id(0)

        @pl.when(step == 0)
        def _():
            copies = [
                pltpu.make_async_copy(ins[i], basis.at[pl.ds(4 * i, 4)], sems.at[i])
                for i in range(n)
            ]
            for copy in copies:
                copy.start()
            acc[...] = jnp.zeros_like(acc)
            for copy in copies:
                copy.wait()

        for j in range(STEP):
            k = step * STEP + j
            acc[col_ref[k]] += jnp.dot(
                basis[row_ref[k]], tile_ref[j], preferred_element_type=F32
            )

        @pl.when(step == count // STEP - 1)
        def _():
            first = pltpu.make_async_copy(acc.at[pl.ds(0, 8)], keep_ref, sems.at[0])
            second = pltpu.make_async_copy(acc.at[pl.ds(8, 8)], send_ref, sems.at[1])
            second.start()
            first.start()
            second.wait()
            first.wait()

    half = jax.ShapeDtypeStruct((8, m, TB), F32)
    return pl.pallas_call(
        body,
        grid_spec=pltpu.PrefetchScalarGridSpec(
            num_scalar_prefetch=2,
            grid=(count // STEP,),
            in_specs=[pl.BlockSpec((STEP, TB, TB), lambda i, *_: (i, 0, 0))] + [ANY] * n,
            out_specs=[ANY, ANY],
            scratch_shapes=[
                pltpu.VMEM((4 * n, m, TB), jnp.bfloat16),
                pltpu.VMEM((16, m, TB), F32),
                pltpu.SemaphoreType.DMA((n,)),
            ],
        ),
        out_shape=[half, half],
        compiler_params=params(),
        cost_estimate=pl.CostEstimate(
            flops=2 * count * TB * TB * m, bytes_accessed=36 * 2**20, transcendentals=0
        ),
        name="first_product",
    )(rows, cols, tiles, *pieces)


def second_product(rows, cols, tiles, pieces, m):
    count = tiles.shape[0]
    n = len(pieces)

    def body(row_ref, col_ref, tile_ref, *rest):
        ins, outs = rest[:n], rest[n : n + 8]
        wide, acc, sems = rest[n + 8 :]
        step = pl.program_id(0)

        @pl.when(step == 0)
        def _():
            copies = [
                pltpu.make_async_copy(ins[i], wide.at[pl.ds(2 * i, 2)], sems.at[i])
                for i in range(n)
            ]
            for copy in copies:
                copy.start()
            acc[...] = jnp.zeros_like(acc)
            for copy in copies:
                copy.wait()

        for j in range(STEP):
            k = step * STEP + j
            acc[row_ref[k]] += lax.dot_general(
                wide[col_ref[k]],
                tile_ref[j],
                (((1,), (1,)), ((), ())),
                preferred_element_type=F32,
            )

        @pl.when(step == count // STEP - 1)
        def _():
            for i in range(8):
                store_coded(outs[i], [acc[4 * i + b] for b in range(4)])

    out = jax.ShapeDtypeStruct((4 * m + PAD, TB), jnp.int16)
    return pl.pallas_call(
        body,
        grid_spec=pltpu.PrefetchScalarGridSpec(
            num_scalar_prefetch=2,
            grid=(count // STEP,),
            in_specs=[pl.BlockSpec((STEP, TB, TB), lambda i, *_: (i, 0, 0))] + [ANY] * n,
            out_specs=[VMEM] * 8,
            scratch_shapes=[
                pltpu.VMEM((2 * n, m, TB), jnp.bfloat16),
                pltpu.VMEM((32, m, TB), F32),
                pltpu.SemaphoreType.DMA((n,)),
            ],
        ),
        out_shape=[out] * 8,
        compiler_params=params(),
        cost_estimate=pl.CostEstimate(
            flops=2 * count * TB * TB * m, bytes_accessed=36 * 2**20, transcendentals=0
        ),
        name="second_product",
    )(rows, cols, tiles, *pieces)


def pair_sum(keep, other, m):
    def body(keep_ref, other_ref, *rest):
        i = pl.program_id(0)
        outs, buf = rest[:4], rest[4]
        for s in range(4):

            @pl.when(i == s)
            def _(s=s):
                store_coded(outs[s], [keep_ref[b] + other_ref[b] for b in range(2)])

    out = jax.ShapeDtypeStruct((2 * m + PAD, TB), jnp.int16)
    block = pl.BlockSpec((2, m, TB), lambda i: (i, 0, 0))
    return pl.pallas_call(
        body,
        grid=(4,),
        in_specs=[block, block],
        out_specs=[VMEM] * 4,
        out_shape=[out] * 4,
        scratch_shapes=[pltpu.VMEM((8, 128), F32)],
        compiler_params=params(),
        name="pair_sum",
    )(keep, other)


def decoded_sum(refs, b, m):
    total = None
    for ref in refs:
        part = ref[b * m : (b + 1) * m, :].astype(F32) * units(ref)[b : b + 1, :]
        total = part if total is None else total + part
    return total


def wide_sum(parts, m):
    def body(*refs):
        for b in range(2):
            refs[4][b] = decoded_sum(refs[:4], b, m).astype(jnp.bfloat16)

    return pl.pallas_call(
        body,
        in_specs=[VMEM] * 4,
        out_specs=VMEM,
        out_shape=jax.ShapeDtypeStruct((2, m, TB), jnp.bfloat16),
        compiler_params=params(),
        name="wide_sum",
    )(*parts)


def middle_sum(parts, m):
    def body(*refs):
        for g in range(2):
            for b in range(4):
                store_coded(
                    refs[8 + 4 * g + b], [decoded_sum(refs[4 * g : 4 * g + 4], b, m)]
                )

    out = jax.ShapeDtypeStruct((m + PAD, TB), jnp.int16)
    return pl.pallas_call(
        body,
        in_specs=[VMEM] * 8,
        out_specs=[VMEM] * 8,
        out_shape=[out] * 8,
        compiler_params=params(),
        name="middle_sum",
    )(*parts)


def last_sum(parts, m):
    def body(*refs):
        for g in range(2):
            refs[8][:, g * TB : (g + 1) * TB] = decoded_sum(
                refs[4 * g : 4 * g + 4], 0, m
            )

    return pl.pallas_call(
        body,
        in_specs=[VMEM] * 8,
        out_specs=VMEM,
        out_shape=jax.ShapeDtypeStruct((m, 2 * TB), F32),
        compiler_params=params(),
        name="last_sum",
    )(*parts)


def spread(value, axis):
    return [value] + [permute(value, axis, hop) for hop in HOPS]


def exchange(pieces, axis):
    return [pieces[0]] + [permute(p, axis, hop) for p, hop in zip(pieces[1:], HOPS)]


def per_device(tile_values, tile_rows, tile_cols, start_basis):
    tiles = tile_values[0, 0]
    rows = tile_rows[0, 0]
    cols = tile_cols[0, 0]
    rank = start_basis.shape[1]
    m = rank // CHUNKS
    z, core = lax.axis_index("row") // 2, lax.axis_index("row") % 2
    x, y = lax.axis_index("col") // 4, lax.axis_index("col") % 4

    odd = rows % 2
    dx, dy = (rows // 8 - x) % 4, (rows // 2 % 4 - y) % 4
    fx, fy = slot_from(dx), slot_from(dy)
    tx, ty = slot_to(dx), slot_to(dy)
    basis_slot = jnp.where(odd == 0, 4 * fy + fx, 16 + 4 * fx + fy)
    image_slot = jnp.where(odd == 0, 4 * tx + ty, 16 + 4 * ty + tx)
    away = jnp.where(cols // 8 == core, 0, 8)
    dz = (cols // 2 % 4 - z) % 4
    partial_slot = away + 2 * slot_to(dz) + cols % 2
    wide_slot = away + 2 * slot_from(dz) + cols % 2

    basis = start_basis.reshape(2, TB, rank).transpose(0, 2, 1)
    images = []
    for chunk in range(CHUNKS):
        own = basis[:, chunk * m : (chunk + 1) * m]
        line_x = jnp.stack(spread(own[0], "x"))
        line_y = jnp.stack(spread(own[1], "y"))
        gathered = spread(line_x, "y") + spread(line_y, "x")
        keep, send = first_product(basis_slot, partial_slot, tiles, gathered, m)
        pieces = pair_sum(keep, permute(send, "core", 1), m)
        wide = spread(wide_sum(exchange(pieces, "z"), m), "z")
        wide = wide + [permute(w, "core", 1) for w in wide]
        parts = second_product(image_slot, wide_slot, tiles, wide, m)
        parts = middle_sum(exchange(parts[:4], "x") + exchange(parts[4:], "y"), m)
        parts = exchange(parts[:4], "y") + exchange(parts[4:], "x")
        images.append(last_sum(parts, m))
    image = jnp.concatenate(images, axis=0)

    gram = lax.dot_general(
        image, image, (((1,), (1,)), ((), ())), precision=lax.Precision.HIGHEST
    )
    gram = gram + permute(gram, "core", 1)
    for axis in ("z", "x", "y"):
        own, up, down, over = spread(gram, axis)
        gram = own + over + (up + down)
    gram = gram / ORDER
    lower = jnp.linalg.cholesky(gram)
    new_basis = jax.scipy.linalg.solve_triangular(lower, image, lower=True).T
    return new_basis, lower.T


def solution(mesh):
    in_specs = (
        P("row", "col", None, None, None),
        P("row", "col", None),
        P("row", "col", None),
        P(("row", "col"), None),
    )
    out_specs = (P(("row", "col"), None), P())
    return jax.shard_map(
        per_device, mesh=mesh, in_specs=in_specs, out_specs=out_specs, check_vma=False
    )
```

```python
import functools

import jax
import jax.numpy as jnp
from jax import lax
from jax.experimental import pallas as pl
from jax.experimental.pallas import tpu as pltpu
from jax.sharding import PartitionSpec as P

ORDER = 131072
TB = 512
CHUNKS = 2
GROUP = 4
PAD = 16
TINY = 1e-30
MIB = 2**20
VMEM = pl.BlockSpec(memory_space=pltpu.VMEM)
ANY = pl.BlockSpec(memory_space=pl.ANY)
F32 = jnp.float32

HOPS = (1, 3, 2)


def permute(value, axis, hop):
    if axis in ("z", "core"):
        name, size = "row", 8
        place = (lambda i: (i + 2 * hop) % 8) if axis == "z" else (lambda i: i ^ 1)
    else:
        name, size = "col", 16
        if axis == "x":
            place = lambda i: (i + 4 * hop) % 16
        else:
            place = lambda i: i // 4 * 4 + (i + hop) % 4
    return lax.ppermute(value, name, [(i, place(i)) for i in range(size)])


def permute_two(value, axes, hop):
    pairs = []
    for i in range(128):
        place = {"z": i // 32, "core": i // 16 % 2, "x": i // 4 % 4, "y": i % 4}
        axis = axes[place["core"]]
        place[axis] = (place[axis] + hop) % 4
        j = (place["z"] * 2 + place["core"]) * 16 + place["x"] * 4 + place["y"]
        pairs.append((i, j))
    return lax.ppermute(value, ("row", "col"), pairs)


def slot_to(distance):
    return jnp.where(distance >= 2, 5 - distance, distance)


def slot_from(distance):
    return slot_to((4 - distance) % 4)


def params(mib):
    return pltpu.CompilerParams(vmem_limit_bytes=mib * MIB)


def exponent(top):
    return jnp.ceil(jnp.log2(jnp.maximum(top, TINY)) + 0.01) - 15.0


def code(value):
    power = exponent(jnp.max(jnp.abs(value), axis=0, keepdims=True))
    return jnp.round(value * jnp.exp2(-power)).astype(jnp.int16), power


def store_coded(ref, blocks):
    powers = []
    for i, value in enumerate(blocks):
        m = value.shape[0]
        ref[i * m : (i + 1) * m, :], power = code(value)
        powers.append(power)
    fill = jnp.zeros((PAD - len(powers), powers[0].shape[1]), F32)
    ref[-PAD:, :] = jnp.concatenate(powers + [fill], axis=0).astype(jnp.int16)


def units(ref):
    return jnp.exp2(ref[-PAD:, :].astype(F32))


def fetched(copies):
    for copy in copies:
        copy.start()
    return copies


def first_product(rows, cols, tiles, pieces, m):
    count = tiles.shape[0]
    n = len(pieces)
    groups = count // GROUP

    def body(row_ref, col_ref, tile_ref, *rest):
        ins, (keep_ref, send_ref, held, basis, acc, sems) = rest[:n], rest[n:]

        def part(g):
            at = pl.ds(g * GROUP, GROUP)
            return pltpu.make_async_copy(tile_ref.at[at], held.at[at], sems.at[n + g])

        sources = [ref.at[pl.ds(0, 4)] for ref in ins]
        copies = fetched(
            [
                pltpu.make_async_copy(sources[i], basis.at[pl.ds(4 * i, 4)], sems.at[i])
                for i in range(n)
            ]
        )
        fetched([part(g) for g in range(groups)])
        acc[...] = jnp.zeros_like(acc)
        for copy in copies:
            copy.wait()

        @pl.loop(0, groups)
        def _(g):
            part(g).wait()
            for j in range(GROUP):
                k = g * GROUP + j
                acc[col_ref[k]] += jnp.dot(
                    basis[row_ref[k]], held[k], preferred_element_type=F32
                )

        outs = fetched(
            [
                pltpu.make_async_copy(acc.at[pl.ds(8, 8)], send_ref, sems.at[0]),
                pltpu.make_async_copy(acc.at[pl.ds(0, 8)], keep_ref, sems.at[1]),
            ]
        )
        for copy in outs:
            copy.wait()

    half = jax.ShapeDtypeStruct((8, m, TB), F32)
    smem = pl.BlockSpec(memory_space=pltpu.SMEM)
    return pl.pallas_call(
        body,
        in_specs=[smem, smem, ANY] + [ANY] * n,
        out_specs=[ANY, ANY],
        scratch_shapes=[
            pltpu.VMEM((count, TB, TB), jnp.bfloat16),
            pltpu.VMEM((4 * n, m, TB), jnp.bfloat16),
            pltpu.VMEM((16, m, TB), F32),
            pltpu.SemaphoreType.DMA((n + groups,)),
        ],
        out_shape=[half, half],
        compiler_params=params(24 + m // 14),
        cost_estimate=pl.CostEstimate(flops=1, bytes_accessed=1, transcendentals=0),
        name="first_product",
    )(rows, cols, tiles, *pieces)


def second_product(rows, cols, tiles, pieces, m):
    count = tiles.shape[0]
    n = len(pieces)
    groups = count // GROUP

    def body(row_ref, col_ref, tile_ref, *rest):
        ins, outs = rest[:n], rest[n : n + 8]
        held, wide, acc, sems = rest[n + 8 :]

        def part(g):
            at = pl.ds(g * GROUP, GROUP)
            return pltpu.make_async_copy(tile_ref.at[at], held.at[at], sems.at[n + g])

        copies = fetched(
            [
                pltpu.make_async_copy(ins[i], wide.at[pl.ds(2 * i, 2)], sems.at[i])
                for i in range(n)
            ]
        )
        fetched([part(g) for g in range(groups)])
        acc[...] = jnp.zeros_like(acc)
        for copy in copies:
            copy.wait()

        @pl.loop(0, groups)
        def _(g):
            part(g).wait()
            for j in range(GROUP):
                k = g * GROUP + j
                acc[row_ref[k]] += lax.dot_general(
                    wide[col_ref[k]],
                    held[k],
                    (((1,), (1,)), ((), ())),
                    preferred_element_type=F32,
                )

        for i in range(8):
            store_coded(outs[i], [acc[4 * i + b] for b in range(4)])

    out = jax.ShapeDtypeStruct((4 * m + PAD, TB), jnp.int16)
    smem = pl.BlockSpec(memory_space=pltpu.SMEM)
    return pl.pallas_call(
        body,
        in_specs=[smem, smem, ANY] + [ANY] * n,
        out_specs=[VMEM] * 8,
        scratch_shapes=[
            pltpu.VMEM((count, TB, TB), jnp.bfloat16),
            pltpu.VMEM((2 * n, m, TB), jnp.bfloat16),
            pltpu.VMEM((32, m, TB), F32),
            pltpu.SemaphoreType.DMA((n + groups,)),
        ],
        out_shape=[out] * 8,
        compiler_params=params(24 + m // 8),
        cost_estimate=pl.CostEstimate(flops=1, bytes_accessed=1, transcendentals=0),
        name="second_product",
    )(rows, cols, tiles, *pieces)


def pair_sum(keep, other, m):
    def body(keep_ref, other_ref, *rest):
        i = pl.program_id(0)
        outs, buf = rest[:4], rest[4]
        for s in range(4):

            @pl.when(i == s)
            def _(s=s):
                store_coded(outs[s], [keep_ref[b] + other_ref[b] for b in range(2)])

    out = jax.ShapeDtypeStruct((2 * m + PAD, TB), jnp.int16)
    block = pl.BlockSpec((2, m, TB), lambda i: (i, 0, 0))
    return pl.pallas_call(
        body,
        grid=(4,),
        in_specs=[block, block],
        out_specs=[VMEM] * 4,
        out_shape=[out] * 4,
        scratch_shapes=[pltpu.VMEM((8, 128), F32)],
        compiler_params=params(16),
        name="pair_sum",
    )(keep, other)


def decoded_sum(refs, b, m):
    total = None
    for ref in refs:
        part = ref[b * m : (b + 1) * m, :].astype(F32) * units(ref)[b : b + 1, :]
        total = part if total is None else total + part
    return total


def wide_sum(parts, m):
    def body(*refs):
        for b in range(2):
            refs[4][b] = decoded_sum(refs[:4], b, m).astype(jnp.bfloat16)

    return pl.pallas_call(
        body,
        in_specs=[VMEM] * 4,
        out_specs=VMEM,
        out_shape=jax.ShapeDtypeStruct((2, m, TB), jnp.bfloat16),
        compiler_params=params(8),
        name="wide_sum",
    )(*parts)


def middle_sum(parts, m):
    def body(*refs):
        for g in range(2):
            for b in range(4):
                store_coded(
                    refs[8 + 4 * g + b], [decoded_sum(refs[4 * g : 4 * g + 4], b, m)]
                )

    out = jax.ShapeDtypeStruct((m + PAD, TB), jnp.int16)
    return pl.pallas_call(
        body,
        in_specs=[VMEM] * 8,
        out_specs=[VMEM] * 8,
        out_shape=[out] * 8,
        compiler_params=params(m // 8),
        name="middle_sum",
    )(*parts)


def last_sum(parts, m):
    def body(*refs):
        for g in range(2):
            refs[8][:, g * TB : (g + 1) * TB] = decoded_sum(
                refs[4 * g : 4 * g + 4], 0, m
            )

    return pl.pallas_call(
        body,
        in_specs=[VMEM] * 8,
        out_specs=VMEM,
        out_shape=jax.ShapeDtypeStruct((m, 2 * TB), F32),
        compiler_params=params(8),
        name="last_sum",
    )(*parts)


def local_gram(core, image):
    rank = image.shape[0]
    half = rank // 2

    def body(core_ref, image_ref, keep_ref, send_ref):
        value = image_ref[...]
        gram = lax.dot_general(
            value,
            value,
            (((1,), (1,)), ((), ())),
            precision=lax.Precision.HIGHEST,
            preferred_element_type=F32,
        )
        first = core_ref[0] == 0
        keep_ref[...] = jnp.where(first, gram[:half], gram[half:])
        send_ref[...] = jnp.where(first, gram[half:], gram[:half])

    out = jax.ShapeDtypeStruct((half, rank), F32)
    return pl.pallas_call(
        body,
        in_specs=[pl.BlockSpec(memory_space=pltpu.SMEM), VMEM],
        out_specs=[VMEM] * 2,
        out_shape=[out] * 2,
        compiler_params=params(8),
        name="local_gram",
    )(core, image)


def inverse_root(value):
    guess = lax.rsqrt(value)
    return guess * (1.5 - 0.5 * value * guess * guess)


def eliminate(panel, at):
    size = panel.shape[0]
    index = lax.broadcasted_iota(jnp.int32, (size, 1), 0)
    done = jnp.zeros_like(panel)
    for j in range(0, size, 2):
        col0, col1 = panel[:, at + j : at + j + 1], panel[:, at + j + 1 : at + j + 2]
        row0, row1 = panel[j : j + 1, :], panel[j + 1 : j + 2, :]
        root0 = inverse_root(col0[j : j + 1, :])
        cross = col0[j + 1 : j + 2, :] * root0
        root1 = inverse_root(col1[j + 1 : j + 2, :] - cross * cross)
        unit0 = row0 * root0
        unit1 = (row1 - cross * unit0) * root1
        part0 = col0 * root0
        part1 = (col1 - cross * part0) * root1
        later = index > j + 1
        part0 = jnp.where(later, part0, 0.0)
        part1 = jnp.where(later, part1, 0.0)
        panel = panel - part0 * unit0 - part1 * unit1
        done = jnp.where(index == j, unit0, jnp.where(index == j + 1, unit1, done))
    return done


def factor(core, mine, other, image):
    rank, count = image.shape
    size = 64

    def body(core_ref, mine_ref, other_ref, image_ref, triangle_ref, basis_ref, work):
        first = core_ref[0] == 0
        a, b = mine_ref[...] * (1.0 / ORDER), other_ref[...] * (1.0 / ORDER)
        work[: rank // 2, :rank] = jnp.where(first, a, b)
        work[rank // 2 :, :rank] = jnp.where(first, b, a)
        row = lax.broadcasted_iota(jnp.int32, (rank, rank), 0)
        col = lax.broadcasted_iota(jnp.int32, (rank, rank), 1)
        work[:, rank:] = jnp.where(row == col, 1.0, 0.0)
        for at in range(0, rank, size):
            done = eliminate(work[at : at + size, :], at)
            work[at : at + size, :] = done
            if at + size < rank:
                work[at + size :, :] -= lax.dot_general(
                    done[:, at + size : rank],
                    done,
                    (((0,), (0,)), ((), ())),
                    precision=lax.Precision.HIGHEST,
                    preferred_element_type=F32,
                )
        triangle_ref[...] = jnp.where(row <= col, work[:, :rank], 0.0)
        basis_ref[...] = lax.dot_general(
            image_ref[...],
            jnp.where(col <= row, work[:, rank:], 0.0),
            (((0,), (1,)), ((), ())),
            precision=lax.Precision.HIGHEST,
            preferred_element_type=F32,
        )

    return pl.pallas_call(
        body,
        in_specs=[pl.BlockSpec(memory_space=pltpu.SMEM)] + [VMEM] * 3,
        out_specs=[VMEM] * 2,
        out_shape=[
            jax.ShapeDtypeStruct((rank, rank), F32),
            jax.ShapeDtypeStruct((count, rank), F32),
        ],
        scratch_shapes=[pltpu.VMEM((rank, 2 * rank), F32)],
        compiler_params=params(16),
        name="factor",
    )(core, mine, other, image)


def spread(value, axis):
    return [value] + [permute(value, axis, hop) for hop in HOPS]


def spread_two(value, axes):
    return [value] + [permute_two(value, axes, hop) for hop in HOPS]


def after(value, *others):
    return lax.optimization_barrier((value, *others))[0]


def exchange(pieces, axis):
    return [pieces[0]] + [permute(p, axis, hop) for p, hop in zip(pieces[1:], HOPS)]


def per_device(tile_values, tile_rows, tile_cols, start_basis):
    tiles = tile_values[0, 0]
    rows = tile_rows[0, 0]
    cols = tile_cols[0, 0]
    rank = start_basis.shape[1]
    m = rank // CHUNKS
    z, core = lax.axis_index("row") // 2, lax.axis_index("row") % 2
    x, y = lax.axis_index("col") // 4, lax.axis_index("col") % 4

    odd = rows % 2
    dx, dy = (rows // 8 - x) % 4, (rows // 2 % 4 - y) % 4
    fx, fy = slot_from(dx), slot_from(dy)
    tx, ty = slot_to(dx), slot_to(dy)
    basis_slot = jnp.where(odd == core, 0, 16) + jnp.where(
        odd == 0, 4 * fy + fx, 4 * fx + fy
    )
    image_slot = jnp.where(odd == 0, 4 * tx + ty, 16 + 4 * ty + tx)
    away = jnp.where(cols // 8 == core, 0, 8)
    dz = (cols // 2 % 4 - z) % 4
    partial_slot = away + 2 * slot_to(dz) + cols % 2
    wide_slot = away + 2 * slot_from(dz) + cols % 2

    basis = start_basis.reshape(2, TB, rank).transpose(0, 2, 1)
    mine = lax.dynamic_index_in_dim(basis, core, 0, keepdims=False)
    other = lax.dynamic_index_in_dim(basis, 1 - core, 0, keepdims=False)
    pair = jnp.stack([mine, permute(other, "core", 1)])
    near = spread_two(pair, "xy")

    def gather(c):
        line = jnp.stack(
            [v[i, c * m : (c + 1) * m] for i in range(2) for v in near]
        )
        plane = spread_two(line, "yx")
        return plane + [permute(v[4:], "core", 1) for v in plane]

    def first(pieces, *others):
        return first_product(
            after(basis_slot, *others), partial_slot, tiles, pieces, m
        )

    def second(wide, *others):
        return second_product(after(image_slot, *others), wide_slot, tiles, wide, m)

    def summed(keep, send, *others):
        return pair_sum(after(keep, *others), permute(send, "core", 1), m)

    def wide_piece(pieces, *others):
        pieces = exchange(pieces, "z")
        return wide_sum([after(pieces[0], *others)] + pieces[1:], m)

    def wide_all(piece):
        wide = spread(piece, "z")
        return wide + [permute(w, "core", 1) for w in wide]

    def halfway(parts, *others):
        parts = exchange(parts[:4], "x") + exchange(parts[4:], "y")
        return middle_sum([after(parts[0], *others)] + parts[1:], m)

    def finished(parts):
        return last_sum(exchange(parts[:4], "y") + exchange(parts[4:], "x"), m)

    basis_a, basis_b = gather(0), gather(1)
    keep_a, send_a = first(basis_a)
    pieces_a = summed(keep_a, send_a)
    keep_b, send_b = first(basis_b, pieces_a[0])
    piece_a = wide_piece(pieces_a, keep_b)
    pieces_b = summed(keep_b, send_b, piece_a)
    parts_a = second(wide_all(piece_a), pieces_b[0])
    piece_b = wide_piece(pieces_b, parts_a[0])
    parts_b = second(wide_all(piece_b))
    blocks_a = halfway(parts_a, parts_b[0])
    blocks_b = halfway(parts_b, blocks_a[0])
    image = jnp.concatenate([finished(blocks_a), finished(blocks_b)], axis=0)

    core = core.astype(jnp.int32).reshape(1)
    keep, send = local_gram(core, image)
    gram = keep + permute(send, "core", 1)
    for axes in ("zx", "xy", "yz"):
        own, up, down, over = [gram] + [permute_two(gram, axes, hop) for hop in HOPS]
        gram = own + over + (up + down)
    triangle, new_basis = factor(core, gram, permute(gram, "core", 1), image)
    return new_basis, triangle


def solution(mesh):
    in_specs = (
        P("row", "col", None, None, None),
        P("row", "col", None),
        P("row", "col", None),
        P(("row", "col"), None),
    )
    out_specs = (P(("row", "col"), None), P())
    return jax.shard_map(
        per_device, mesh=mesh, in_specs=in_specs, out_specs=out_specs, check_vma=False
    )
```

```python
import functools

import jax
import jax.numpy as jnp
from jax import lax
from jax.experimental import pallas as pl
from jax.experimental.pallas import tpu as pltpu
from jax.sharding import PartitionSpec as P

ORDER = 131072
TB = 512
CHUNKS = 2
GROUP = 4
PAD = 16
TINY = 1e-30
MIB = 2**20
VMEM = pl.BlockSpec(memory_space=pltpu.VMEM)
ANY = pl.BlockSpec(memory_space=pl.ANY)
F32 = jnp.float32

HOPS = (1, 3, 2)


def permute(value, axis, hop):
    if axis in ("z", "core"):
        name, size = "row", 8
        place = (lambda i: (i + 2 * hop) % 8) if axis == "z" else (lambda i: i ^ 1)
    else:
        name, size = "col", 16
        if axis == "x":
            place = lambda i: (i + 4 * hop) % 16
        else:
            place = lambda i: i // 4 * 4 + (i + hop) % 4
    return lax.ppermute(value, name, [(i, place(i)) for i in range(size)])


def permute_two(value, axes, hop):
    pairs = []
    for i in range(128):
        place = {"z": i // 32, "core": i // 16 % 2, "x": i // 4 % 4, "y": i % 4}
        axis = axes[place["core"]]
        place[axis] = (place[axis] + hop) % 4
        j = (place["z"] * 2 + place["core"]) * 16 + place["x"] * 4 + place["y"]
        pairs.append((i, j))
    return lax.ppermute(value, ("row", "col"), pairs)


def slot_to(distance):
    return jnp.where(distance >= 2, 5 - distance, distance)


def slot_from(distance):
    return slot_to((4 - distance) % 4)


def params(mib):
    return pltpu.CompilerParams(vmem_limit_bytes=mib * MIB)


def exponent(top):
    return jnp.ceil(jnp.log2(jnp.maximum(top, TINY)) + 0.01) - 15.0


def code(value):
    power = exponent(jnp.max(jnp.abs(value), axis=0, keepdims=True))
    return jnp.round(value * jnp.exp2(-power)).astype(jnp.int16), power


def store_coded(ref, blocks):
    powers = []
    for i, value in enumerate(blocks):
        m = value.shape[0]
        ref[i * m : (i + 1) * m, :], power = code(value)
        powers.append(power)
    fill = jnp.zeros((PAD - len(powers), powers[0].shape[1]), F32)
    ref[-PAD:, :] = jnp.concatenate(powers + [fill], axis=0).astype(jnp.int16)


def units(ref):
    return jnp.exp2(ref[-PAD:, :].astype(F32))


def fetched(copies):
    for copy in copies:
        copy.start()
    return copies


def first_product(rows, cols, tiles, pieces, m):
    count = tiles.shape[0]
    n = len(pieces)
    groups = count // GROUP

    def body(row_ref, col_ref, tile_ref, *rest):
        ins, (keep_ref, low_ref, high_ref, held, basis, acc, sems) = rest[:n], rest[n:]

        def part(g):
            at = pl.ds(g * GROUP, GROUP)
            return pltpu.make_async_copy(tile_ref.at[at], held.at[at], sems.at[n + g])

        copies = fetched(
            [
                pltpu.make_async_copy(ins[i], basis.at[pl.ds(8 * i, 8)], sems.at[i])
                for i in range(n)
            ]
        )
        fetched([part(g) for g in range(groups)])
        acc[...] = jnp.zeros_like(acc)
        for copy in copies:
            copy.wait()

        @pl.loop(0, groups)
        def _(g):
            part(g).wait()
            for j in range(GROUP):
                k = g * GROUP + j
                acc[col_ref[k]] += jnp.dot(
                    basis[row_ref[k]], held[k], preferred_element_type=F32
                )

        out = pltpu.make_async_copy(acc.at[pl.ds(0, 8)], keep_ref, sems.at[0])
        out.start()
        store_coded(low_ref, [acc[8 + b] for b in range(4)])
        store_coded(high_ref, [acc[12 + b] for b in range(4)])
        out.wait()

    half = jax.ShapeDtypeStruct((4 * m + PAD, TB), jnp.int16)
    smem = pl.BlockSpec(memory_space=pltpu.SMEM)
    return pl.pallas_call(
        body,
        in_specs=[smem, smem, ANY] + [ANY] * n,
        out_specs=[ANY, VMEM, VMEM],
        scratch_shapes=[
            pltpu.VMEM((count, TB, TB), jnp.bfloat16),
            pltpu.VMEM((8 * n, m, TB), jnp.bfloat16),
            pltpu.VMEM((16, m, TB), F32),
            pltpu.SemaphoreType.DMA((n + groups,)),
        ],
        out_shape=[jax.ShapeDtypeStruct((8, m, TB), F32), half, half],
        compiler_params=params(24 + m // 14),
        cost_estimate=pl.CostEstimate(flops=1, bytes_accessed=1, transcendentals=0),
        name="first_product",
    )(rows, cols, tiles, *pieces)


def second_product(rows, cols, tiles, pieces, m):
    count = tiles.shape[0]
    n = len(pieces)
    groups = count // GROUP

    def body(row_ref, col_ref, tile_ref, *rest):
        ins, outs = rest[:n], rest[n : n + 4]
        held, wide, acc, sems = rest[n + 4 :]

        def part(g):
            at = pl.ds(g * GROUP, GROUP)
            return pltpu.make_async_copy(tile_ref.at[at], held.at[at], sems.at[n + g])

        copies = fetched(
            [
                pltpu.make_async_copy(ins[i], wide.at[pl.ds(2 * i, 2)], sems.at[i])
                for i in range(n)
            ]
        )
        fetched([part(g) for g in range(groups)])
        acc[...] = jnp.zeros_like(acc)
        for copy in copies:
            copy.wait()

        @pl.loop(0, groups)
        def _(g):
            part(g).wait()
            for j in range(GROUP):
                k = g * GROUP + j
                acc[row_ref[k]] += lax.dot_general(
                    wide[col_ref[k]],
                    held[k],
                    (((1,), (1,)), ((), ())),
                    preferred_element_type=F32,
                )

        for i in range(4):
            store_coded(outs[i], [acc[8 * i + b] for b in range(8)])

    out = jax.ShapeDtypeStruct((8 * m + PAD, TB), jnp.int16)
    smem = pl.BlockSpec(memory_space=pltpu.SMEM)
    return pl.pallas_call(
        body,
        in_specs=[smem, smem, ANY] + [ANY] * n,
        out_specs=[VMEM] * 4,
        scratch_shapes=[
            pltpu.VMEM((count, TB, TB), jnp.bfloat16),
            pltpu.VMEM((2 * n, m, TB), jnp.bfloat16),
            pltpu.VMEM((32, m, TB), F32),
            pltpu.SemaphoreType.DMA((n + groups,)),
        ],
        out_shape=[out] * 4,
        compiler_params=params(24 + m // 8),
        cost_estimate=pl.CostEstimate(flops=1, bytes_accessed=1, transcendentals=0),
        name="second_product",
    )(rows, cols, tiles, *pieces)


def decoded_sum(refs, b, m):
    total = None
    for ref in refs:
        part = ref[b * m : (b + 1) * m, :].astype(F32) * units(ref)[b : b + 1, :]
        total = part if total is None else total + part
    return total


def pair_sum(keep, low, high, m):
    def body(keep_ref, low_ref, high_ref, *outs):
        for s in range(4):
            other = low_ref if s < 2 else high_ref
            store_coded(
                outs[s],
                [
                    keep_ref[2 * s + b] + decoded_sum([other], 2 * (s % 2) + b, m)
                    for b in range(2)
                ],
            )

    out = jax.ShapeDtypeStruct((2 * m + PAD, TB), jnp.int16)
    return pl.pallas_call(
        body,
        in_specs=[VMEM] * 3,
        out_specs=[VMEM] * 4,
        out_shape=[out] * 4,
        compiler_params=params(16),
        name="pair_sum",
    )(keep, low, high)


def wide_sum(parts, m):
    def body(*refs):
        for b in range(2):
            refs[4][b] = decoded_sum(refs[:4], b, m).astype(jnp.bfloat16)

    return pl.pallas_call(
        body,
        in_specs=[VMEM] * 4,
        out_specs=VMEM,
        out_shape=jax.ShapeDtypeStruct((2, m, TB), jnp.bfloat16),
        compiler_params=params(8),
        cost_estimate=pl.CostEstimate(flops=2 * 10**10, bytes_accessed=1, transcendentals=0),
        name="wide_sum",
    )(*parts)


def middle_sum(parts, m):
    def body(*refs):
        for s in range(4):
            store_coded(
                refs[4 + s], [decoded_sum(refs[:4], 2 * s + b, m) for b in range(2)]
            )

    out = jax.ShapeDtypeStruct((2 * m + PAD, TB), jnp.int16)
    return pl.pallas_call(
        body,
        in_specs=[VMEM] * 4,
        out_specs=[VMEM] * 4,
        out_shape=[out] * 4,
        compiler_params=params(m // 8),
        name="middle_sum",
    )(*parts)


def last_sum(parts, m):
    def body(*refs):
        for b in range(2):
            refs[4][:, b * TB : (b + 1) * TB] = decoded_sum(refs[:4], b, m)

    return pl.pallas_call(
        body,
        in_specs=[VMEM] * 4,
        out_specs=VMEM,
        out_shape=jax.ShapeDtypeStruct((m, 2 * TB), F32),
        compiler_params=params(8),
        name="last_sum",
    )(*parts)


def local_gram(core, image):
    rank = image.shape[0]
    half = rank // 2

    def body(core_ref, image_ref, keep_ref, send_ref):
        value = image_ref[...]
        gram = lax.dot_general(
            value,
            value,
            (((1,), (1,)), ((), ())),
            precision=lax.Precision.HIGHEST,
            preferred_element_type=F32,
        )
        first = core_ref[0] == 0
        keep_ref[...] = jnp.where(first, gram[:half], gram[half:])
        send_ref[...] = jnp.where(first, gram[half:], gram[:half])

    out = jax.ShapeDtypeStruct((half, rank), F32)
    return pl.pallas_call(
        body,
        in_specs=[pl.BlockSpec(memory_space=pltpu.SMEM), VMEM],
        out_specs=[VMEM] * 2,
        out_shape=[out] * 2,
        compiler_params=params(8),
        name="local_gram",
    )(core, image)


def full_dot(a, b, at_a, at_b):
    return lax.dot_general(
        a,
        b,
        (((at_a,), (at_b,)), ((), ())),
        precision=lax.Precision.HIGHEST,
        preferred_element_type=F32,
    )


def inverse_root(value):
    guess = lax.rsqrt(value)
    return guess * (1.5 - 0.5 * value * guess * guess)


def eliminate(block):
    size = block.shape[0]
    index = lax.broadcasted_iota(jnp.int32, (size, 1), 0)
    row = lax.broadcasted_iota(jnp.int32, (size, size), 0)
    col = lax.broadcasted_iota(jnp.int32, (size, size), 1)
    work = jnp.concatenate([block, jnp.where(row == col, 1.0, 0.0)], axis=1)
    rows = []
    for j in range(0, size, 2):
        col0, col1 = work[:, j : j + 1], work[:, j + 1 : j + 2]
        row0, row1 = work[j : j + 1, :], work[j + 1 : j + 2, :]
        root0 = inverse_root(col0[j : j + 1, :])
        cross = col0[j + 1 : j + 2, :] * root0
        root1 = inverse_root(col1[j + 1 : j + 2, :] - cross * cross)
        unit0 = row0 * root0
        unit1 = (row1 - cross * unit0) * root1
        rows += [unit0, unit1]
        part0 = col0 * root0
        part1 = (col1 - cross * part0) * root1
        later = index > j + 1
        work = work - jnp.where(later, part0, 0.0) * unit0 - jnp.where(later, part1, 0.0) * unit1
    return jnp.where(col <= row, jnp.concatenate(rows, axis=0)[:, size:], 0.0)


def factor(core, mine, other, image):
    rank, count = image.shape
    size = 64

    def body(core_ref, mine_ref, other_ref, image_ref, triangle_ref, basis_ref, work):
        first = core_ref[0] == 0
        a, b = mine_ref[...] * (1.0 / ORDER), other_ref[...] * (1.0 / ORDER)
        work[: rank // 2, :rank] = jnp.where(first, a, b)
        work[rank // 2 :, :rank] = jnp.where(first, b, a)
        row = lax.broadcasted_iota(jnp.int32, (rank, rank), 0)
        col = lax.broadcasted_iota(jnp.int32, (rank, rank), 1)
        work[:, rank:] = jnp.where(row == col, 1.0, 0.0)
        for at in range(0, rank, size):
            panel = work[at : at + size, :]
            done = full_dot(eliminate(panel[:, at : at + size]), panel, 1, 0)
            work[at : at + size, :] = done
            if at + size < rank:
                work[at + size :, :] -= full_dot(done[:, at + size : rank], done, 0, 0)
        triangle_ref[...] = jnp.where(row <= col, work[:, :rank], 0.0)
        inverse = jnp.where(col <= row, work[:, rank:], 0.0)
        basis_ref[...] = full_dot(image_ref[...], inverse, 0, 1)

    return pl.pallas_call(
        body,
        in_specs=[pl.BlockSpec(memory_space=pltpu.SMEM)] + [VMEM] * 3,
        out_specs=[VMEM] * 2,
        out_shape=[
            jax.ShapeDtypeStruct((rank, rank), F32),
            jax.ShapeDtypeStruct((count, rank), F32),
        ],
        scratch_shapes=[pltpu.VMEM((rank, 2 * rank), F32)],
        compiler_params=params(16),
        name="factor",
    )(core, mine, other, image)


def spread(value, axis):
    return [value] + [permute(value, axis, hop) for hop in HOPS]


def spread_two(value, axes):
    return [value] + [permute_two(value, axes, hop) for hop in HOPS]


def exchange_two(pieces, axes):
    return [pieces[0]] + [permute_two(p, axes, h) for p, h in zip(pieces[1:], HOPS)]


def after(value, *others):
    return lax.optimization_barrier((value, *others))[0]


def exchange(pieces, axis):
    return [pieces[0]] + [permute(p, axis, hop) for p, hop in zip(pieces[1:], HOPS)]


def per_device(tile_values, tile_rows, tile_cols, start_basis):
    tiles = tile_values[0, 0]
    rows = tile_rows[0, 0]
    cols = tile_cols[0, 0]
    rank = start_basis.shape[1]
    m = rank // CHUNKS
    z, core = lax.axis_index("row") // 2, lax.axis_index("row") % 2
    x, y = lax.axis_index("col") // 4, lax.axis_index("col") % 4

    odd = rows % 2
    dx, dy = (rows // 8 - x) % 4, (rows // 2 % 4 - y) % 4
    near, far = jnp.where(core == 0, dx, dy), jnp.where(core == 0, dy, dx)
    basis_slot = 8 * slot_from(far) + 2 * slot_from(near) + odd
    image_slot = 8 * slot_to(near) + 2 * slot_to(far) + odd
    away = jnp.where(cols // 8 == core, 0, 8)
    dz = (cols // 2 % 4 - z) % 4
    partial_slot = away + 2 * slot_to(dz) + cols % 2
    wide_slot = away + 2 * slot_from(dz) + cols % 2

    basis = start_basis.reshape(2, TB, rank).transpose(0, 2, 1)
    close = spread_two(basis, "xy")

    def gathered(c):
        line = jnp.stack([v[:, c * m : (c + 1) * m] for v in close])
        return spread_two(line.reshape(8, m, TB), "yx")

    def first(pieces, *others):
        return first_product(
            after(basis_slot, *others), partial_slot, tiles, pieces, m
        )

    def second(wide, *others):
        return second_product(after(image_slot, *others), wide_slot, tiles, wide, m)

    def summed(keep, low, high, *others):
        return pair_sum(
            after(keep, *others), permute(low, "core", 1), permute(high, "core", 1), m
        )

    def wide_piece(pieces, *others):
        pieces = exchange(pieces, "z")
        return wide_sum([after(pieces[0], *others)] + pieces[1:], m)

    def wide_all(wide):
        return wide + [permute(w, "core", 1) for w in wide]

    def halfway(parts, *others):
        parts = exchange_two(parts, "xy")
        return middle_sum([after(parts[0], *others)] + parts[1:], m)

    def finished(parts):
        return last_sum(exchange_two(parts, "yx"), m)

    basis_a, basis_b = gathered(0), gathered(1)
    halves_a = first(basis_a)
    pieces_a = summed(*halves_a)
    halves_b = first(basis_b, pieces_a[0])
    piece_a = wide_piece(pieces_a, halves_b[0])
    wide_a = spread(piece_a, "z")
    pieces_b = summed(*halves_b, wide_a[1], wide_a[2], wide_a[3])
    parts_a = second(wide_all(wide_a), pieces_b[0])
    wide_b = spread(wide_piece(pieces_b, parts_a[0]), "z")
    parts_b = second(wide_all(wide_b), parts_a[0])
    blocks_a = halfway(parts_a, parts_b[0])
    blocks_b = halfway(parts_b, blocks_a[0])
    image = jnp.concatenate([finished(blocks_a), finished(blocks_b)], axis=0)

    core = core.astype(jnp.int32).reshape(1)
    keep, send = local_gram(core, image)
    gram = keep + permute(send, "core", 1)
    for axes in ("zx", "xy", "yz"):
        own, up, down, over = [gram] + [permute_two(gram, axes, hop) for hop in HOPS]
        gram = own + over + (up + down)
    triangle, new_basis = factor(core, gram, permute(gram, "core", 1), image)
    return new_basis, triangle


def solution(mesh):
    in_specs = (
        P("row", "col", None, None, None),
        P("row", "col", None),
        P("row", "col", None),
        P(("row", "col"), None),
    )
    out_specs = (P(("row", "col"), None), P())
    return jax.shard_map(
        per_device, mesh=mesh, in_specs=in_specs, out_specs=out_specs, check_vma=False
    )
```

```python
import functools

import jax
import jax.numpy as jnp
from jax import lax
from jax.experimental import pallas as pl
from jax.experimental.pallas import tpu as pltpu
from jax.sharding import PartitionSpec as P

ORDER = 131072
TB = 512
CHUNKS = 2
GROUP = 4
PAD = 16
PIVOTS = 8
TINY = 1e-30
MIB = 2**20
VMEM = pl.BlockSpec(memory_space=pltpu.VMEM)
ANY = pl.BlockSpec(memory_space=pl.ANY)
F32 = jnp.float32

HOPS = (1, 3, 2)


def permute(value, axis, hop):
    if axis in ("z", "core"):
        name, size = "row", 8
        place = (lambda i: (i + 2 * hop) % 8) if axis == "z" else (lambda i: i ^ 1)
    else:
        name, size = "col", 16
        if axis == "x":
            place = lambda i: (i + 4 * hop) % 16
        else:
            place = lambda i: i // 4 * 4 + (i + hop) % 4
    return lax.ppermute(value, name, [(i, place(i)) for i in range(size)])


def permute_two(value, axes, hop):
    pairs = []
    for i in range(128):
        place = {"z": i // 32, "core": i // 16 % 2, "x": i // 4 % 4, "y": i % 4}
        axis = axes[place["core"]]
        place[axis] = (place[axis] + hop) % 4
        j = (place["z"] * 2 + place["core"]) * 16 + place["x"] * 4 + place["y"]
        pairs.append((i, j))
    return lax.ppermute(value, ("row", "col"), pairs)


def slot_to(distance):
    return jnp.where(distance >= 2, 5 - distance, distance)


def slot_from(distance):
    return slot_to((4 - distance) % 4)


def params(mib):
    return pltpu.CompilerParams(vmem_limit_bytes=mib * MIB)


def exponent(top):
    return jnp.ceil(jnp.log2(jnp.maximum(top, TINY)) + 0.01) - 15.0


def code(value):
    power = exponent(jnp.max(jnp.abs(value), axis=0, keepdims=True))
    return jnp.round(value * jnp.exp2(-power)).astype(jnp.int16), power


def store_coded(ref, blocks):
    powers = []
    for i, value in enumerate(blocks):
        m = value.shape[0]
        ref[i * m : (i + 1) * m, :], power = code(value)
        powers.append(power)
    fill = jnp.zeros((PAD - len(powers), powers[0].shape[1]), F32)
    ref[-PAD:, :] = jnp.concatenate(powers + [fill], axis=0).astype(jnp.int16)


def units(ref):
    return jnp.exp2(ref[-PAD:, :].astype(F32))


def fetched(copies):
    for copy in copies:
        copy.start()
    return copies


def first_product(rows, cols, tiles, pieces, m, fetch):
    count = tiles.shape[0]
    n = len(pieces)
    groups = count // GROUP

    def body(row_ref, col_ref, tile_ref, *rest):
        ins, (keep_ref, low_ref, high_ref, basis, acc, sems, *held) = rest[:n], rest[n:]

        def part(g):
            at = pl.ds(g * GROUP, GROUP)
            return pltpu.make_async_copy(
                tile_ref.at[at], held[0].at[at], sems.at[n + g]
            )

        source = held[0] if fetch else tile_ref

        copies = fetched(
            [
                pltpu.make_async_copy(ins[i], basis.at[pl.ds(8 * i, 8)], sems.at[i])
                for i in range(n)
            ]
        )
        if fetch:
            fetched([part(g) for g in range(groups)])
        acc[...] = jnp.zeros_like(acc)
        for copy in copies:
            copy.wait()

        @pl.loop(0, groups)
        def _(g):
            if fetch:
                part(g).wait()
            for j in range(GROUP):
                k = g * GROUP + j
                acc[col_ref[k]] += jnp.dot(
                    basis[row_ref[k]], source[k], preferred_element_type=F32
                )

        out = pltpu.make_async_copy(acc.at[pl.ds(0, 8)], keep_ref, sems.at[0])
        out.start()
        store_coded(low_ref, [acc[8 + b] for b in range(4)])
        store_coded(high_ref, [acc[12 + b] for b in range(4)])
        out.wait()

    half = jax.ShapeDtypeStruct((4 * m + PAD, TB), jnp.int16)
    smem = pl.BlockSpec(memory_space=pltpu.SMEM)
    return pl.pallas_call(
        body,
        in_specs=[smem, smem, ANY if fetch else VMEM] + [ANY] * n,
        out_specs=[ANY, VMEM, VMEM],
        scratch_shapes=[
            pltpu.VMEM((8 * n, m, TB), jnp.bfloat16),
            pltpu.VMEM((16, m, TB), F32),
            pltpu.SemaphoreType.DMA((n + groups,)),
        ]
        + [pltpu.VMEM(tiles.shape, tiles.dtype)] * fetch,
        out_shape=[jax.ShapeDtypeStruct((8, m, TB), F32), half, half],
        compiler_params=params(14 + 20 * fetch),
        cost_estimate=pl.CostEstimate(flops=1, bytes_accessed=1, transcendentals=0),
        name="first_product",
    )(rows, cols, tiles, *pieces)


def second_product(rows, cols, tiles, pieces, m):
    count = tiles.shape[0]
    n = len(pieces)
    groups = count // GROUP
    starts = [sum(p.shape[0] for p in pieces[:i]) for i in range(n)]

    def body(row_ref, col_ref, tile_ref, *rest):
        ins, outs = rest[:n], rest[n : n + 4]
        wide, acc, sems = rest[n + 4 :]

        copies = fetched(
            [
                pltpu.make_async_copy(
                    ins[i], wide.at[pl.ds(starts[i], ins[i].shape[0])], sems.at[i]
                )
                for i in range(n)
            ]
        )
        acc[...] = jnp.zeros_like(acc)
        for copy in copies:
            copy.wait()

        @pl.loop(0, groups)
        def _(g):
            for j in range(GROUP):
                k = g * GROUP + j
                acc[row_ref[k]] += lax.dot_general(
                    wide[col_ref[k]],
                    tile_ref[k],
                    (((1,), (1,)), ((), ())),
                    preferred_element_type=F32,
                )

        for i in range(4):
            store_coded(outs[i], [acc[8 * i + b] for b in range(8)])

    out = jax.ShapeDtypeStruct((8 * m + PAD, TB), jnp.int16)
    smem = pl.BlockSpec(memory_space=pltpu.SMEM)
    return pl.pallas_call(
        body,
        in_specs=[smem, smem, VMEM] + [ANY] * n,
        out_specs=[VMEM] * 4,
        scratch_shapes=[
            pltpu.VMEM((16, m, TB), jnp.bfloat16),
            pltpu.VMEM((32, m, TB), F32),
            pltpu.SemaphoreType.DMA((n,)),
        ],
        out_shape=[out] * 4,
        compiler_params=params(24),
        cost_estimate=pl.CostEstimate(flops=1, bytes_accessed=1, transcendentals=0),
        name="second_product",
    )(rows, cols, tiles, *pieces)


def decoded_sum(refs, b, m):
    total = None
    for ref in refs:
        part = ref[b * m : (b + 1) * m, :].astype(F32) * units(ref)[b : b + 1, :]
        total = part if total is None else total + part
    return total


def pair_sum(keep, low, high, m):
    def body(keep_ref, low_ref, high_ref, *outs):
        for s in range(4):
            other = low_ref if s < 2 else high_ref
            store_coded(
                outs[s],
                [
                    keep_ref[2 * s + b] + decoded_sum([other], 2 * (s % 2) + b, m)
                    for b in range(2)
                ],
            )

    out = jax.ShapeDtypeStruct((2 * m + PAD, TB), jnp.int16)
    return pl.pallas_call(
        body,
        in_specs=[VMEM] * 3,
        out_specs=[VMEM] * 4,
        out_shape=[out] * 4,
        compiler_params=params(16),
        name="pair_sum",
    )(keep, low, high)


def wide_sum(parts, m):
    def body(*refs):
        for b in range(2):
            refs[4][b] = decoded_sum(refs[:4], b, m).astype(jnp.bfloat16)

    return pl.pallas_call(
        body,
        in_specs=[VMEM] * 4,
        out_specs=VMEM,
        out_shape=jax.ShapeDtypeStruct((2, m, TB), jnp.bfloat16),
        compiler_params=params(8),
        cost_estimate=pl.CostEstimate(flops=2 * 10**10, bytes_accessed=1, transcendentals=0),
        name="wide_sum",
    )(*parts)


def middle_sum(parts, m):
    def body(*refs):
        for s in range(4):
            store_coded(
                refs[4 + s], [decoded_sum(refs[:4], 2 * s + b, m) for b in range(2)]
            )

    out = jax.ShapeDtypeStruct((2 * m + PAD, TB), jnp.int16)
    return pl.pallas_call(
        body,
        in_specs=[VMEM] * 4,
        out_specs=[VMEM] * 4,
        out_shape=[out] * 4,
        compiler_params=params(m // 8),
        name="middle_sum",
    )(*parts)


def last_sum(parts, m):
    def body(*refs):
        for b in range(2):
            refs[4][:, b * TB : (b + 1) * TB] = decoded_sum(refs[:4], b, m)

    return pl.pallas_call(
        body,
        in_specs=[VMEM] * 4,
        out_specs=VMEM,
        out_shape=jax.ShapeDtypeStruct((m, 2 * TB), F32),
        compiler_params=params(8),
        name="last_sum",
    )(*parts)


def local_gram(core, image):
    rank = image.shape[0]
    half = rank // 2

    def body(core_ref, image_ref, keep_ref, send_ref):
        value = image_ref[...]
        gram = lax.dot_general(
            value,
            value,
            (((1,), (1,)), ((), ())),
            precision=lax.Precision.HIGHEST,
            preferred_element_type=F32,
        )
        first = core_ref[0] == 0
        keep_ref[...] = jnp.where(first, gram[:half], gram[half:])
        send_ref[...] = jnp.where(first, gram[half:], gram[:half])

    out = jax.ShapeDtypeStruct((half, rank), F32)
    return pl.pallas_call(
        body,
        in_specs=[pl.BlockSpec(memory_space=pltpu.SMEM), VMEM],
        out_specs=[VMEM] * 2,
        out_shape=[out] * 2,
        compiler_params=params(8),
        name="local_gram",
    )(core, image)


def full_dot(a, b, at_a, at_b):
    return lax.dot_general(
        a,
        b,
        (((at_a,), (at_b,)), ((), ())),
        precision=lax.Precision.HIGHEST,
        preferred_element_type=F32,
    )


def eliminate(block):
    size = block.shape[0]
    index = lax.broadcasted_iota(jnp.int32, (size, 1), 0)
    row = lax.broadcasted_iota(jnp.int32, (size, size), 0)
    col = lax.broadcasted_iota(jnp.int32, (size, size), 1)
    work = jnp.concatenate([block, jnp.where(row == col, 1.0, 0.0)], axis=1)
    rows = []
    for j in range(0, size, PIVOTS):
        cols = [
            jnp.broadcast_to(work[:, j + i : j + i + 1], work.shape)
            for i in range(PIVOTS)
        ]
        units, parts = [], []
        for i in range(PIVOTS):
            unit, part = work[j + i : j + i + 1, :], cols[i]
            for p in range(i):
                entry = parts[p][j + i : j + i + 1, :]
                unit = unit - entry * units[p]
                part = part - entry * parts[p]
            root = lax.rsqrt(part[j + i : j + i + 1, :])
            units.append(unit * root)
            parts.append(part * root)
        rows += units
        later = index >= j + PIVOTS
        if j + PIVOTS < size:
            for unit, part in zip(units, parts):
                work = work - jnp.where(later, part, 0.0) * unit
    return jnp.where(col <= row, jnp.concatenate(rows, axis=0)[:, size:], 0.0)


def factor(core, mine, other, image):
    rank, count = image.shape
    size = 64

    def body(core_ref, mine_ref, other_ref, image_ref, triangle_ref, basis_ref, work):
        first = core_ref[0] == 0
        a, b = mine_ref[...] * (1.0 / ORDER), other_ref[...] * (1.0 / ORDER)
        work[: rank // 2, :rank] = jnp.where(first, a, b)
        work[rank // 2 :, :rank] = jnp.where(first, b, a)
        row = lax.broadcasted_iota(jnp.int32, (rank, rank), 0)
        col = lax.broadcasted_iota(jnp.int32, (rank, rank), 1)
        work[:, rank:] = jnp.where(row == col, 1.0, 0.0)
        for at in range(0, rank, size):
            panel = work[at : at + size, :]
            done = full_dot(eliminate(panel[:, at : at + size]), panel, 1, 0)
            work[at : at + size, :] = done
            if at + size < rank:
                work[at + size :, :] -= full_dot(done[:, at + size : rank], done, 0, 0)
        triangle_ref[...] = jnp.where(row <= col, work[:, :rank], 0.0)
        inverse = jnp.where(col <= row, work[:, rank:], 0.0)
        basis_ref[...] = full_dot(image_ref[...], inverse, 0, 1)

    return pl.pallas_call(
        body,
        in_specs=[pl.BlockSpec(memory_space=pltpu.SMEM)] + [VMEM] * 3,
        out_specs=[VMEM] * 2,
        out_shape=[
            jax.ShapeDtypeStruct((rank, rank), F32),
            jax.ShapeDtypeStruct((count, rank), F32),
        ],
        scratch_shapes=[pltpu.VMEM((rank, 2 * rank), F32)],
        compiler_params=params(16),
        name="factor",
    )(core, mine, other, image)


def spread(value, axis):
    return [value] + [permute(value, axis, hop) for hop in HOPS]


def spread_two(value, axes):
    return [value] + [permute_two(value, axes, hop) for hop in HOPS]


def exchange_two(pieces, axes):
    return [pieces[0]] + [permute_two(p, axes, h) for p, h in zip(pieces[1:], HOPS)]


def after(value, *others):
    return lax.optimization_barrier((value, *others))[0]


def exchange(pieces, axis):
    return [pieces[0]] + [permute(p, axis, hop) for p, hop in zip(pieces[1:], HOPS)]


def per_device(tile_values, tile_rows, tile_cols, start_basis):
    tiles = tile_values[0, 0]
    rows = tile_rows[0, 0]
    cols = tile_cols[0, 0]
    rank = start_basis.shape[1]
    m = rank // CHUNKS
    z, core = lax.axis_index("row") // 2, lax.axis_index("row") % 2
    x, y = lax.axis_index("col") // 4, lax.axis_index("col") % 4

    odd = rows % 2
    dx, dy = (rows // 8 - x) % 4, (rows // 2 % 4 - y) % 4
    near, far = jnp.where(core == 0, dx, dy), jnp.where(core == 0, dy, dx)
    basis_slot = 8 * slot_from(far) + 2 * slot_from(near) + odd
    image_slot = 8 * slot_to(near) + 2 * slot_to(far) + odd
    away = jnp.where(cols // 8 == core, 0, 8)
    dz = (cols // 2 % 4 - z) % 4
    partial_slot = away + 2 * slot_to(dz) + cols % 2
    wide_slot = jnp.where(away == 0, 2 * slot_from(dz), 8 + 2 * (4 - slot_from(dz)) % 8)
    wide_slot = wide_slot + cols % 2

    basis = start_basis.reshape(2, TB, rank).transpose(0, 2, 1)

    def lined(c, *others):
        part = after(basis[:, c * m : (c + 1) * m], *others)
        return jnp.concatenate(spread_two(part, "xy"))

    def gathered(line):
        return spread_two(line, "yx")

    def first(pieces, fetch, *others):
        slots = after(basis_slot, *others)
        return first_product(slots, partial_slot, tiles, pieces, m, fetch)

    def second(wide, *others):
        return second_product(after(image_slot, *others), wide_slot, tiles, wide, m)

    def summed(keep, low, high, *others):
        return pair_sum(
            after(keep, *others), permute(low, "core", 1), permute(high, "core", 1), m
        )

    def wide_piece(pieces, *others):
        pieces = exchange(pieces, "z")
        return wide_sum([after(pieces[0], *others)] + pieces[1:], m)

    def wide_all(wide, *others):
        pairs = [(wide[0], wide[3]), (wide[2], wide[1])]
        pairs = [after(jnp.concatenate(p), *others) for p in pairs]
        return wide + [permute(p, "core", 1) for p in pairs]

    def halfway(parts, *others):
        return middle_sum([after(parts[0], *others)] + parts[1:], m)

    def finished(parts):
        return last_sum(exchange_two(parts, "yx"), m)

    line_a = lined(0)
    line_b = lined(1, line_a)
    basis_a, basis_b = gathered(line_a), gathered(line_b)
    halves_a = first(basis_a, True)
    pieces_a = summed(*halves_a)
    halves_b = first(basis_b, False, pieces_a[0])
    piece_a = wide_piece(pieces_a, halves_b[0])
    wide_a = spread(piece_a, "z")
    pieces_b = summed(*halves_b, wide_a[3])
    parts_a = second(wide_all(wide_a), pieces_b[0])
    wide_b = spread(wide_piece(pieces_b, parts_a[0]), "z")
    parts_a = exchange_two(parts_a, "xy")
    parts_b = second(wide_all(wide_b, parts_a[1], parts_a[2]))
    parts_b = exchange_two(parts_b, "xy")
    blocks_a = halfway(parts_a, parts_b[0])
    blocks_b = halfway(parts_b, blocks_a[0])
    image = jnp.concatenate([finished(blocks_a), finished(blocks_b)], axis=0)

    core = core.astype(jnp.int32).reshape(1)
    keep, send = local_gram(core, image)
    gram = keep + permute(send, "core", 1)
    for axes in ("zx", "xy", "yz"):
        own, up, down, over = [gram] + [permute_two(gram, axes, hop) for hop in HOPS]
        gram = own + over + (up + down)
    triangle, new_basis = factor(core, gram, permute(gram, "core", 1), image)
    return new_basis, triangle


def solution(mesh):
    in_specs = (
        P("row", "col", None, None, None),
        P("row", "col", None),
        P("row", "col", None),
        P(("row", "col"), None),
    )
    out_specs = (P(("row", "col"), None), P())
    return jax.shard_map(
        per_device, mesh=mesh, in_specs=in_specs, out_specs=out_specs, check_vma=False
    )
```

```python
import functools

import jax
import jax.numpy as jnp
from jax import lax
from jax.experimental import pallas as pl
from jax.experimental.pallas import tpu as pltpu
from jax.sharding import PartitionSpec as P

ORDER = 131072
TB = 512
CHUNKS = 2
GROUP = 8
RUN = 20
PAD = 16
PIVOTS = 8
TINY = 1e-30
MIB = 2**20
VMEM = pl.BlockSpec(memory_space=pltpu.VMEM)
ANY = pl.BlockSpec(memory_space=pl.ANY)
F32 = jnp.float32

HOPS = (1, 3, 2)


def permute(value, axis, hop):
    if axis in ("z", "core"):
        name, size = "row", 8
        place = (lambda i: (i + 2 * hop) % 8) if axis == "z" else (lambda i: i ^ 1)
    else:
        name, size = "col", 16
        if axis == "x":
            place = lambda i: (i + 4 * hop) % 16
        else:
            place = lambda i: i // 4 * 4 + (i + hop) % 4
    return lax.ppermute(value, name, [(i, place(i)) for i in range(size)])


def permute_two(value, axes, hop):
    pairs = []
    for i in range(128):
        place = {"z": i // 32, "core": i // 16 % 2, "x": i // 4 % 4, "y": i % 4}
        axis = axes[place["core"]]
        place[axis] = (place[axis] + hop) % 4
        j = (place["z"] * 2 + place["core"]) * 16 + place["x"] * 4 + place["y"]
        pairs.append((i, j))
    return lax.ppermute(value, ("row", "col"), pairs)


def slot_to(distance):
    return jnp.where(distance >= 2, 5 - distance, distance)


def slot_from(distance):
    return slot_to((4 - distance) % 4)


def params(mib):
    return pltpu.CompilerParams(vmem_limit_bytes=mib * MIB)


def exponent(top):
    return jnp.ceil(jnp.log2(jnp.maximum(top, TINY)) + 0.01) - 15.0


def code(value):
    high = jnp.max(value, axis=0, keepdims=True)
    low = jnp.min(value, axis=0, keepdims=True)
    power = exponent(jnp.maximum(high, -low))
    whole = jnp.round(value * jnp.exp2(-power)).astype(jnp.int32)
    return whole.astype(jnp.int16), power


def store_coded(ref, blocks):
    powers = []
    for i, value in enumerate(blocks):
        m = value.shape[0]
        ref[i * m : (i + 1) * m, :], power = code(value)
        powers.append(power)
    fill = jnp.zeros((PAD - len(powers), powers[0].shape[1]), F32)
    ref[-PAD:, :] = jnp.concatenate(powers + [fill], axis=0).astype(jnp.int16)


def units(ref):
    return jnp.exp2(ref[-PAD:, :].astype(F32))


def fetched(copies):
    for copy in copies:
        copy.start()
    return copies


def first_product(rows, cols, tiles, pieces, m, fetch):
    count = tiles.shape[0]
    n = len(pieces)
    groups = count // GROUP

    def body(row_ref, col_ref, tile_ref, *rest):
        ins, (keep_ref, low_ref, high_ref, basis, acc, sems, *held) = rest[:n], rest[n:]

        def part(g):
            at = pl.ds(g * GROUP, GROUP)
            return pltpu.make_async_copy(
                tile_ref.at[at], held[0].at[at], sems.at[n + g]
            )

        source = held[0] if fetch else tile_ref

        copies = fetched(
            [
                pltpu.make_async_copy(ins[i], basis.at[pl.ds(8 * i, 8)], sems.at[i])
                for i in range(n)
            ]
        )
        if fetch:
            fetched([part(g) for g in range(groups)])
        acc[...] = jnp.zeros_like(acc)
        for copy in copies:
            copy.wait()

        run = GROUP if fetch else RUN

        @pl.loop(0, count // run)
        def _(g):
            if fetch:
                part(g).wait()
            for j in range(run):
                k = g * run + j
                acc[col_ref[k]] += jnp.dot(
                    basis[row_ref[k]], source[k], preferred_element_type=F32
                )

        out = pltpu.make_async_copy(acc.at[pl.ds(0, 8)], keep_ref, sems.at[0])
        out.start()
        store_coded(low_ref, [acc[8 + b] for b in range(4)])
        store_coded(high_ref, [acc[12 + b] for b in range(4)])
        out.wait()

    half = jax.ShapeDtypeStruct((4 * m + PAD, TB), jnp.int16)
    smem = pl.BlockSpec(memory_space=pltpu.SMEM)
    return pl.pallas_call(
        body,
        in_specs=[smem, smem, ANY if fetch else VMEM] + [ANY] * n,
        out_specs=[ANY, VMEM, VMEM],
        scratch_shapes=[
            pltpu.VMEM((8 * n, m, TB), jnp.bfloat16),
            pltpu.VMEM((16, m, TB), F32),
            pltpu.SemaphoreType.DMA((n + groups,)),
        ]
        + [pltpu.VMEM(tiles.shape, tiles.dtype)] * fetch,
        out_shape=[jax.ShapeDtypeStruct((8, m, TB), F32), half, half],
        compiler_params=params(14 + 20 * fetch),
        cost_estimate=pl.CostEstimate(flops=1, bytes_accessed=1, transcendentals=0),
        name="first_product",
    )(rows, cols, tiles, *pieces)


def second_product(rows, cols, tiles, pieces, m):
    count = tiles.shape[0]
    n = len(pieces)
    groups = count // GROUP
    starts = [sum(p.shape[0] for p in pieces[:i]) for i in range(n)]

    def body(row_ref, col_ref, tile_ref, *rest):
        ins, outs = rest[:n], rest[n : n + 4]
        wide, acc, sems = rest[n + 4 :]

        copies = fetched(
            [
                pltpu.make_async_copy(
                    ins[i], wide.at[pl.ds(starts[i], ins[i].shape[0])], sems.at[i]
                )
                for i in range(n)
            ]
        )
        acc[...] = jnp.zeros_like(acc)
        for copy in copies:
            copy.wait()

        @pl.loop(0, groups)
        def _(g):
            for j in range(GROUP):
                k = g * GROUP + j
                acc[row_ref[k]] += lax.dot_general(
                    wide[col_ref[k]],
                    tile_ref[k],
                    (((1,), (1,)), ((), ())),
                    preferred_element_type=F32,
                )

        for i in range(4):
            store_coded(outs[i], [acc[8 * i + b] for b in range(8)])

    out = jax.ShapeDtypeStruct((8 * m + PAD, TB), jnp.int16)
    smem = pl.BlockSpec(memory_space=pltpu.SMEM)
    return pl.pallas_call(
        body,
        in_specs=[smem, smem, VMEM] + [ANY] * n,
        out_specs=[VMEM] * 4,
        scratch_shapes=[
            pltpu.VMEM((16, m, TB), jnp.bfloat16),
            pltpu.VMEM((32, m, TB), F32),
            pltpu.SemaphoreType.DMA((n,)),
        ],
        out_shape=[out] * 4,
        compiler_params=params(24),
        cost_estimate=pl.CostEstimate(flops=1, bytes_accessed=1, transcendentals=0),
        name="second_product",
    )(rows, cols, tiles, *pieces)


def decoded_sum(refs, b, m):
    total = None
    for ref in refs:
        part = ref[b * m : (b + 1) * m, :].astype(F32) * units(ref)[b : b + 1, :]
        total = part if total is None else total + part
    return total


def pair_sum(keep, low, high, m):
    def body(keep_ref, low_ref, high_ref, *outs):
        for s in range(4):
            other = low_ref if s < 2 else high_ref
            store_coded(
                outs[s],
                [
                    keep_ref[2 * s + b] + decoded_sum([other], 2 * (s % 2) + b, m)
                    for b in range(2)
                ],
            )

    out = jax.ShapeDtypeStruct((2 * m + PAD, TB), jnp.int16)
    return pl.pallas_call(
        body,
        in_specs=[VMEM] * 3,
        out_specs=[VMEM] * 4,
        out_shape=[out] * 4,
        compiler_params=params(16),
        name="pair_sum",
    )(keep, low, high)


def wide_sum(parts, m):
    def body(*refs):
        for b in range(2):
            refs[4][b] = decoded_sum(refs[:4], b, m).astype(jnp.bfloat16)

    return pl.pallas_call(
        body,
        in_specs=[VMEM] * 4,
        out_specs=VMEM,
        out_shape=jax.ShapeDtypeStruct((2, m, TB), jnp.bfloat16),
        compiler_params=params(8),
        cost_estimate=pl.CostEstimate(flops=2 * 10**10, bytes_accessed=1, transcendentals=0),
        name="wide_sum",
    )(*parts)


def middle_sum(parts, m):
    def body(*refs):
        for s in range(4):
            store_coded(
                refs[4 + s], [decoded_sum(refs[:4], 2 * s + b, m) for b in range(2)]
            )

    out = jax.ShapeDtypeStruct((2 * m + PAD, TB), jnp.int16)
    return pl.pallas_call(
        body,
        in_specs=[VMEM] * 4,
        out_specs=[VMEM] * 4,
        out_shape=[out] * 4,
        compiler_params=params(m // 8),
        name="middle_sum",
    )(*parts)


def last_sum(parts, m):
    def body(*refs):
        for b in range(2):
            refs[4][:, b * TB : (b + 1) * TB] = decoded_sum(refs[:4], b, m)

    return pl.pallas_call(
        body,
        in_specs=[VMEM] * 4,
        out_specs=VMEM,
        out_shape=jax.ShapeDtypeStruct((m, 2 * TB), F32),
        compiler_params=params(8),
        name="last_sum",
    )(*parts)


def local_gram(core, image):
    rank = image.shape[0]
    half = rank // 2

    def body(core_ref, image_ref, keep_ref, send_ref):
        value = image_ref[...]
        gram = lax.dot_general(
            value,
            value,
            (((1,), (1,)), ((), ())),
            precision=lax.Precision.HIGHEST,
            preferred_element_type=F32,
        )
        first = core_ref[0] == 0
        keep_ref[...] = jnp.where(first, gram[:half], gram[half:])
        send_ref[...] = jnp.where(first, gram[half:], gram[:half])

    out = jax.ShapeDtypeStruct((half, rank), F32)
    return pl.pallas_call(
        body,
        in_specs=[pl.BlockSpec(memory_space=pltpu.SMEM), VMEM],
        out_specs=[VMEM] * 2,
        out_shape=[out] * 2,
        compiler_params=params(8),
        name="local_gram",
    )(core, image)


def full_dot(a, b, at_a, at_b):
    return lax.dot_general(
        a,
        b,
        (((at_a,), (at_b,)), ((), ())),
        precision=lax.Precision.HIGHEST,
        preferred_element_type=F32,
    )


def eliminate(block):
    size = block.shape[0]
    index = lax.broadcasted_iota(jnp.int32, (size, 1), 0)
    row = lax.broadcasted_iota(jnp.int32, (size, size), 0)
    col = lax.broadcasted_iota(jnp.int32, (size, size), 1)
    work = jnp.concatenate([block, jnp.where(row == col, 1.0, 0.0)], axis=1)
    rows = []
    for j in range(0, size, PIVOTS):
        cols = [
            jnp.broadcast_to(work[:, j + i : j + i + 1], work.shape)
            for i in range(PIVOTS)
        ]
        units, parts = [], []
        for i in range(PIVOTS):
            unit, part = work[j + i : j + i + 1, :], cols[i]
            for p in range(i):
                entry = parts[p][j + i : j + i + 1, :]
                unit = unit - entry * units[p]
                part = part - entry * parts[p]
            root = lax.rsqrt(part[j + i : j + i + 1, :])
            units.append(unit * root)
            parts.append(part * root)
        rows += units
        later = index >= j + PIVOTS
        if j + PIVOTS < size:
            for unit, part in zip(units, parts):
                work = work - jnp.where(later, part, 0.0) * unit
    return jnp.where(col <= row, jnp.concatenate(rows, axis=0)[:, size:], 0.0)


def factor(core, mine, other, image):
    rank, count = image.shape
    size = 64

    def body(core_ref, mine_ref, other_ref, image_ref, triangle_ref, basis_ref, work):
        first = core_ref[0] == 0
        a, b = mine_ref[...] * (1.0 / ORDER), other_ref[...] * (1.0 / ORDER)
        work[: rank // 2, :rank] = jnp.where(first, a, b)
        work[rank // 2 :, :rank] = jnp.where(first, b, a)
        row = lax.broadcasted_iota(jnp.int32, (rank, rank), 0)
        col = lax.broadcasted_iota(jnp.int32, (rank, rank), 1)
        work[:, rank:] = jnp.where(row == col, 1.0, 0.0)
        for at in range(0, rank, size):
            panel = work[at : at + size, :]
            done = full_dot(eliminate(panel[:, at : at + size]), panel, 1, 0)
            work[at : at + size, :] = done
            if at + size < rank:
                work[at + size :, :] -= full_dot(done[:, at + size : rank], done, 0, 0)
        triangle_ref[...] = jnp.where(row <= col, work[:, :rank], 0.0)
        inverse = jnp.where(col <= row, work[:, rank:], 0.0)
        basis_ref[...] = full_dot(image_ref[...], inverse, 0, 1)

    return pl.pallas_call(
        body,
        in_specs=[pl.BlockSpec(memory_space=pltpu.SMEM)] + [VMEM] * 3,
        out_specs=[VMEM] * 2,
        out_shape=[
            jax.ShapeDtypeStruct((rank, rank), F32),
            jax.ShapeDtypeStruct((count, rank), F32),
        ],
        scratch_shapes=[pltpu.VMEM((rank, 2 * rank), F32)],
        compiler_params=params(16),
        name="factor",
    )(core, mine, other, image)


def spread(value, axis):
    return [value] + [permute(value, axis, hop) for hop in HOPS]


def spread_two(value, axes):
    return [value] + [permute_two(value, axes, hop) for hop in HOPS]


def exchange_two(pieces, axes):
    return [pieces[0]] + [permute_two(p, axes, h) for p, h in zip(pieces[1:], HOPS)]


def after(value, *others):
    return lax.optimization_barrier((value, *others))[0]


def exchange(pieces, axis):
    return [pieces[0]] + [permute(p, axis, hop) for p, hop in zip(pieces[1:], HOPS)]


def per_device(tile_values, tile_rows, tile_cols, start_basis):
    tiles = tile_values[0, 0]
    rows = tile_rows[0, 0]
    cols = tile_cols[0, 0]
    rank = start_basis.shape[1]
    m = rank // CHUNKS
    z, core = lax.axis_index("row") // 2, lax.axis_index("row") % 2
    x, y = lax.axis_index("col") // 4, lax.axis_index("col") % 4

    odd = rows % 2
    dx, dy = (rows // 8 - x) % 4, (rows // 2 % 4 - y) % 4
    near, far = jnp.where(core == 0, dx, dy), jnp.where(core == 0, dy, dx)
    basis_slot = 8 * slot_from(far) + 2 * slot_from(near) + odd
    image_slot = 8 * slot_to(near) + 2 * slot_to(far) + odd
    away = jnp.where(cols // 8 == core, 0, 8)
    dz = (cols // 2 % 4 - z) % 4
    partial_slot = away + 2 * slot_to(dz) + cols % 2
    wide_slot = jnp.where(away == 0, 2 * slot_from(dz), 8 + 2 * (4 - slot_from(dz)) % 8)
    wide_slot = wide_slot + cols % 2

    basis = start_basis.reshape(2, TB, rank).transpose(0, 2, 1)

    def lined(c, *others):
        part = after(basis[:, c * m : (c + 1) * m], *others)
        return jnp.concatenate(spread_two(part, "xy"))

    def gathered(line):
        return spread_two(line, "yx")

    def first(pieces, fetch, *others):
        slots = after(basis_slot, *others)
        return first_product(slots, partial_slot, tiles, pieces, m, fetch)

    def second(wide, *others):
        return second_product(after(image_slot, *others), wide_slot, tiles, wide, m)

    def summed(keep, low, high, *others):
        return pair_sum(
            after(keep, *others), permute(low, "core", 1), permute(high, "core", 1), m
        )

    def wide_piece(pieces, *others):
        pieces = exchange(pieces, "z")
        return wide_sum([after(pieces[0], *others)] + pieces[1:], m)

    def wide_all(wide, *others):
        pairs = [(wide[0], wide[3]), (wide[2], wide[1])]
        pairs = [after(jnp.concatenate(p), *others) for p in pairs]
        return wide + [permute(p, "core", 1) for p in pairs]

    def halfway(parts, *others):
        return middle_sum([after(parts[0], *others)] + parts[1:], m)

    def finished(parts):
        return last_sum(exchange_two(parts, "yx"), m)

    line_a = lined(0)
    line_b = lined(1, line_a)
    basis_a, basis_b = gathered(line_a), gathered(line_b)
    halves_a = first(basis_a, True)
    pieces_a = summed(*halves_a)
    halves_b = first(basis_b, False, pieces_a[0])
    piece_a = wide_piece(pieces_a, halves_b[0])
    wide_a = spread(piece_a, "z")
    pieces_b = summed(*halves_b, wide_a[3])
    parts_a = second(wide_all(wide_a), pieces_b[0])
    wide_b = spread(wide_piece(pieces_b, parts_a[0]), "z")
    parts_a = exchange_two(parts_a, "xy")
    parts_b = second(wide_all(wide_b, parts_a[1], parts_a[2]))
    parts_b = exchange_two(parts_b, "xy")
    blocks_a = halfway(parts_a, parts_b[0])
    blocks_b = halfway(parts_b, blocks_a[0])
    image = jnp.concatenate([finished(blocks_a), finished(blocks_b)], axis=0)

    core = core.astype(jnp.int32).reshape(1)
    keep, send = local_gram(core, image)
    gram = keep + permute(send, "core", 1)
    for axes in ("zx", "xy", "yz"):
        own, up, down, over = [gram] + [permute_two(gram, axes, hop) for hop in HOPS]
        gram = own + over + (up + down)
    triangle, new_basis = factor(core, gram, permute(gram, "core", 1), image)
    return new_basis, triangle


def solution(mesh):
    in_specs = (
        P("row", "col", None, None, None),
        P("row", "col", None),
        P("row", "col", None),
        P(("row", "col"), None),
    )
    out_specs = (P(("row", "col"), None), P())
    return jax.shard_map(
        per_device, mesh=mesh, in_specs=in_specs, out_specs=out_specs, check_vma=False
    )
```

```python
import functools

import jax
import jax.numpy as jnp
from jax import lax
from jax.experimental import pallas as pl
from jax.experimental.pallas import tpu as pltpu
from jax.sharding import PartitionSpec as P

ORDER = 131072
TB = 512
CHUNKS = 2
GROUP = 8
RUN = 20
PAD = 16
PIVOTS = 8
TINY = 1e-30
MIB = 2**20
VMEM = pl.BlockSpec(memory_space=pltpu.VMEM)
ANY = pl.BlockSpec(memory_space=pl.ANY)
F32 = jnp.float32

HOPS = (1, 3, 2)


def permute(value, axis, hop):
    if axis in ("z", "core"):
        name, size = "row", 8
        place = (lambda i: (i + 2 * hop) % 8) if axis == "z" else (lambda i: i ^ 1)
    else:
        name, size = "col", 16
        if axis == "x":
            place = lambda i: (i + 4 * hop) % 16
        else:
            place = lambda i: i // 4 * 4 + (i + hop) % 4
    return lax.ppermute(value, name, [(i, place(i)) for i in range(size)])


def permute_two(value, axes, hop):
    pairs = []
    for i in range(128):
        place = {"z": i // 32, "core": i // 16 % 2, "x": i // 4 % 4, "y": i % 4}
        axis = axes[place["core"]]
        place[axis] = (place[axis] + hop) % 4
        j = (place["z"] * 2 + place["core"]) * 16 + place["x"] * 4 + place["y"]
        pairs.append((i, j))
    return lax.ppermute(value, ("row", "col"), pairs)


def slot_to(distance):
    return jnp.where(distance >= 2, 5 - distance, distance)


def slot_from(distance):
    return slot_to((4 - distance) % 4)


def params(mib):
    return pltpu.CompilerParams(vmem_limit_bytes=mib * MIB)


def exponent(top):
    return jnp.ceil(jnp.log2(jnp.maximum(top, TINY)) + 0.01) - 15.0


def code(value):
    high = jnp.max(value, axis=0, keepdims=True)
    low = jnp.min(value, axis=0, keepdims=True)
    power = exponent(jnp.maximum(high, -low))
    whole = jnp.round(value * jnp.exp2(-power)).astype(jnp.int32)
    return whole.astype(jnp.int16), power


def store_coded(ref, blocks):
    powers = []
    for i, value in enumerate(blocks):
        m = value.shape[0]
        ref[i * m : (i + 1) * m, :], power = code(value)
        powers.append(power)
    fill = jnp.zeros((PAD - len(powers), powers[0].shape[1]), F32)
    ref[-PAD:, :] = jnp.concatenate(powers + [fill], axis=0).astype(jnp.int16)


def units(ref):
    return jnp.exp2(ref[-PAD:, :].astype(F32))


def fetched(copies):
    for copy in copies:
        copy.start()
    return copies


def first_product(rows, cols, tiles, pieces, m, fetch):
    count = tiles.shape[0]
    n = len(pieces)
    groups = count // GROUP

    def body(row_ref, col_ref, tile_ref, *rest):
        ins, (keep_ref, low_ref, high_ref, basis, acc, sems, *held) = rest[:n], rest[n:]

        def part(g):
            at = pl.ds(g * GROUP, GROUP)
            return pltpu.make_async_copy(
                tile_ref.at[at], held[0].at[at], sems.at[n + g]
            )

        source = held[0] if fetch else tile_ref

        copies = fetched(
            [
                pltpu.make_async_copy(ins[i], basis.at[pl.ds(8 * i, 8)], sems.at[i])
                for i in range(n)
            ]
        )
        if fetch:
            fetched([part(g) for g in range(groups)])
        acc[...] = jnp.zeros_like(acc)
        for copy in copies:
            copy.wait()

        run = GROUP if fetch else RUN

        @pl.loop(0, count // run)
        def _(g):
            if fetch:
                part(g).wait()
            for j in range(run):
                k = g * run + j
                acc[col_ref[k]] += jnp.dot(
                    basis[row_ref[k]], source[k], preferred_element_type=F32
                )

        out = pltpu.make_async_copy(acc.at[pl.ds(0, 8)], keep_ref, sems.at[0])
        out.start()
        store_coded(low_ref, [acc[8 + b] for b in range(4)])
        store_coded(high_ref, [acc[12 + b] for b in range(4)])
        out.wait()

    half = jax.ShapeDtypeStruct((4 * m + PAD, TB), jnp.int16)
    smem = pl.BlockSpec(memory_space=pltpu.SMEM)
    return pl.pallas_call(
        body,
        in_specs=[smem, smem, ANY if fetch else VMEM] + [ANY] * n,
        out_specs=[ANY, VMEM, VMEM],
        scratch_shapes=[
            pltpu.VMEM((8 * n, m, TB), jnp.bfloat16),
            pltpu.VMEM((16, m, TB), F32),
            pltpu.SemaphoreType.DMA((n + groups,)),
        ]
        + [pltpu.VMEM(tiles.shape, tiles.dtype)] * fetch,
        out_shape=[jax.ShapeDtypeStruct((8, m, TB), F32), half, half],
        compiler_params=params(14 + 20 * fetch),
        cost_estimate=pl.CostEstimate(flops=1, bytes_accessed=1, transcendentals=0),
        name="first_product",
    )(rows, cols, tiles, *pieces)


def second_product(rows, cols, tiles, pieces, m):
    count = tiles.shape[0]
    n = len(pieces)
    groups = count // GROUP
    starts = [sum(p.shape[0] for p in pieces[:i]) for i in range(n)]

    def body(row_ref, col_ref, tile_ref, *rest):
        ins, outs = rest[:n], rest[n : n + 4]
        wide, acc, sems = rest[n + 4 :]

        copies = fetched(
            [
                pltpu.make_async_copy(
                    ins[i], wide.at[pl.ds(starts[i], ins[i].shape[0])], sems.at[i]
                )
                for i in range(n)
            ]
        )
        acc[...] = jnp.zeros_like(acc)
        for copy in copies:
            copy.wait()

        @pl.loop(0, groups)
        def _(g):
            for j in range(GROUP):
                k = g * GROUP + j
                acc[row_ref[k]] += lax.dot_general(
                    wide[col_ref[k]],
                    tile_ref[k],
                    (((1,), (1,)), ((), ())),
                    preferred_element_type=F32,
                )

        for i in range(4):
            store_coded(outs[i], [acc[8 * i + b] for b in range(8)])

    out = jax.ShapeDtypeStruct((8 * m + PAD, TB), jnp.int16)
    smem = pl.BlockSpec(memory_space=pltpu.SMEM)
    return pl.pallas_call(
        body,
        in_specs=[smem, smem, VMEM] + [ANY] * n,
        out_specs=[VMEM] * 4,
        scratch_shapes=[
            pltpu.VMEM((16, m, TB), jnp.bfloat16),
            pltpu.VMEM((32, m, TB), F32),
            pltpu.SemaphoreType.DMA((n,)),
        ],
        out_shape=[out] * 4,
        compiler_params=params(24),
        cost_estimate=pl.CostEstimate(flops=1, bytes_accessed=1, transcendentals=0),
        name="second_product",
    )(rows, cols, tiles, *pieces)


def decoded_sum(refs, b, m):
    total = None
    for ref in refs:
        part = ref[b * m : (b + 1) * m, :].astype(F32) * units(ref)[b : b + 1, :]
        total = part if total is None else total + part
    return total


def pair_sum(keep, low, high, m):
    def body(keep_ref, low_ref, high_ref, *outs):
        for s in range(4):
            other = low_ref if s < 2 else high_ref
            store_coded(
                outs[s],
                [
                    keep_ref[2 * s + b] + decoded_sum([other], 2 * (s % 2) + b, m)
                    for b in range(2)
                ],
            )

    out = jax.ShapeDtypeStruct((2 * m + PAD, TB), jnp.int16)
    return pl.pallas_call(
        body,
        in_specs=[VMEM] * 3,
        out_specs=[VMEM] * 4,
        out_shape=[out] * 4,
        compiler_params=params(16),
        name="pair_sum",
    )(keep, low, high)


def wide_sum(parts, m):
    def body(*refs):
        for b in range(2):
            refs[4][b] = decoded_sum(refs[:4], b, m).astype(jnp.bfloat16)

    return pl.pallas_call(
        body,
        in_specs=[VMEM] * 4,
        out_specs=VMEM,
        out_shape=jax.ShapeDtypeStruct((2, m, TB), jnp.bfloat16),
        compiler_params=params(8),
        cost_estimate=pl.CostEstimate(flops=2 * 10**10, bytes_accessed=1, transcendentals=0),
        name="wide_sum",
    )(*parts)


def middle_sum(parts, m):
    def body(*refs):
        for s in range(4):
            store_coded(
                refs[4 + s], [decoded_sum(refs[:4], 2 * s + b, m) for b in range(2)]
            )

    out = jax.ShapeDtypeStruct((2 * m + PAD, TB), jnp.int16)
    return pl.pallas_call(
        body,
        in_specs=[VMEM] * 4,
        out_specs=[VMEM] * 4,
        out_shape=[out] * 4,
        compiler_params=params(m // 8),
        name="middle_sum",
    )(*parts)


def last_sum(parts, m):
    def body(*refs):
        for b in range(2):
            refs[4][:, b * TB : (b + 1) * TB] = decoded_sum(refs[:4], b, m)

    return pl.pallas_call(
        body,
        in_specs=[VMEM] * 4,
        out_specs=VMEM,
        out_shape=jax.ShapeDtypeStruct((m, 2 * TB), F32),
        compiler_params=params(8),
        name="last_sum",
    )(*parts)


def local_gram(core, image):
    rank = image.shape[0]
    half = rank // 2

    def body(core_ref, image_ref, keep_ref, send_ref):
        value = image_ref[...]
        gram = lax.dot_general(
            value,
            value,
            (((1,), (1,)), ((), ())),
            precision=lax.Precision.HIGHEST,
            preferred_element_type=F32,
        )
        first = core_ref[0] == 0
        keep_ref[...] = jnp.where(first, gram[:half], gram[half:])
        send_ref[...] = jnp.where(first, gram[half:], gram[:half])

    out = jax.ShapeDtypeStruct((half, rank), F32)
    return pl.pallas_call(
        body,
        in_specs=[pl.BlockSpec(memory_space=pltpu.SMEM), VMEM],
        out_specs=[VMEM] * 2,
        out_shape=[out] * 2,
        compiler_params=params(8),
        name="local_gram",
    )(core, image)


def full_dot(a, b, at_a, at_b):
    return lax.dot_general(
        a,
        b,
        (((at_a,), (at_b,)), ((), ())),
        precision=lax.Precision.HIGHEST,
        preferred_element_type=F32,
    )


def eliminate(block):
    size = block.shape[0]
    index = lax.broadcasted_iota(jnp.int32, (size, 1), 0)
    row = lax.broadcasted_iota(jnp.int32, (size, size), 0)
    col = lax.broadcasted_iota(jnp.int32, (size, size), 1)
    work = jnp.concatenate([block, jnp.where(row == col, 1.0, 0.0)], axis=1)
    rows = []
    for j in range(0, size, PIVOTS):
        cols = [
            jnp.broadcast_to(work[:, j + i : j + i + 1], work.shape)
            for i in range(PIVOTS)
        ]
        units, parts = [], []
        for i in range(PIVOTS):
            unit, part = work[j + i : j + i + 1, :], cols[i]
            for p in range(i):
                entry = parts[p][j + i : j + i + 1, :]
                unit = unit - entry * units[p]
                part = part - entry * parts[p]
            root = lax.rsqrt(part[j + i : j + i + 1, :])
            units.append(unit * root)
            parts.append(part * root)
        rows += units
        later = index >= j + PIVOTS
        if j + PIVOTS < size:
            for unit, part in zip(units, parts):
                work = work - jnp.where(later, part, 0.0) * unit
    return jnp.where(col <= row, jnp.concatenate(rows, axis=0)[:, size:], 0.0)


def factor(core, mine, other, image):
    rank, count = image.shape
    size = 64

    def body(core_ref, mine_ref, other_ref, image_ref, triangle_ref, basis_ref, work):
        first = core_ref[0] == 0
        a, b = mine_ref[...] * (1.0 / ORDER), other_ref[...] * (1.0 / ORDER)
        work[: rank // 2, :rank] = jnp.where(first, a, b)
        work[rank // 2 :, :rank] = jnp.where(first, b, a)
        row = lax.broadcasted_iota(jnp.int32, (rank, rank), 0)
        col = lax.broadcasted_iota(jnp.int32, (rank, rank), 1)
        work[:, rank:] = jnp.where(row == col, 1.0, 0.0)
        for at in range(0, rank, size):
            panel = work[at : at + size, :]
            done = full_dot(eliminate(panel[:, at : at + size]), panel, 1, 0)
            work[at : at + size, :] = done
            if at + size < rank:
                work[at + size :, :] -= full_dot(done[:, at + size : rank], done, 0, 0)
        triangle_ref[...] = jnp.where(row <= col, work[:, :rank], 0.0)
        inverse = jnp.where(col <= row, work[:, rank:], 0.0)
        basis_ref[...] = full_dot(image_ref[...], inverse, 0, 1)

    return pl.pallas_call(
        body,
        in_specs=[pl.BlockSpec(memory_space=pltpu.SMEM)] + [VMEM] * 3,
        out_specs=[VMEM] * 2,
        out_shape=[
            jax.ShapeDtypeStruct((rank, rank), F32),
            jax.ShapeDtypeStruct((count, rank), F32),
        ],
        scratch_shapes=[pltpu.VMEM((rank, 2 * rank), F32)],
        compiler_params=params(16),
        name="factor",
    )(core, mine, other, image)


def spread(value, axis):
    return [value] + [permute(value, axis, hop) for hop in HOPS]


def spread_two(value, axes):
    return [value] + [permute_two(value, axes, hop) for hop in HOPS]


def exchange_two(pieces, axes):
    return [pieces[0]] + [permute_two(p, axes, h) for p, h in zip(pieces[1:], HOPS)]


def after(value, *others):
    return lax.optimization_barrier((value, *others))[0]


def exchange(pieces, axis):
    return [pieces[0]] + [permute(p, axis, hop) for p, hop in zip(pieces[1:], HOPS)]


def per_device(tile_values, tile_rows, tile_cols, start_basis):
    tiles = tile_values[0, 0]
    rows = tile_rows[0, 0]
    cols = tile_cols[0, 0]
    rank = start_basis.shape[1]
    m = rank // CHUNKS
    z, core = lax.axis_index("row") // 2, lax.axis_index("row") % 2
    x, y = lax.axis_index("col") // 4, lax.axis_index("col") % 4

    odd = rows % 2
    dx, dy = (rows // 8 - x) % 4, (rows // 2 % 4 - y) % 4
    near, far = jnp.where(core == 0, dx, dy), jnp.where(core == 0, dy, dx)
    basis_slot = 8 * slot_from(far) + 2 * slot_from(near) + odd
    image_slot = 8 * slot_to(near) + 2 * slot_to(far) + odd
    away = jnp.where(cols // 8 == core, 0, 8)
    dz = (cols // 2 % 4 - z) % 4
    partial_slot = away + 2 * slot_to(dz) + cols % 2
    wide_slot = jnp.where(away == 0, 2 * slot_from(dz), 8 + 2 * (4 - slot_from(dz)) % 8)
    wide_slot = wide_slot + cols % 2

    basis = start_basis.reshape(2, TB, rank).transpose(0, 2, 1)

    def lined(c, *others):
        part = after(basis[:, c * m : (c + 1) * m], *others)
        return jnp.concatenate(spread_two(part, "xy"))

    def gathered(line):
        return spread_two(line, "yx")

    def first(pieces, fetch, *others):
        slots = after(basis_slot, *others)
        return first_product(slots, partial_slot, tiles, pieces, m, fetch)

    def second(wide, *others):
        return second_product(after(image_slot, *others), wide_slot, tiles, wide, m)

    def summed(keep, low, high, *others):
        return pair_sum(
            after(keep, *others), permute(low, "core", 1), permute(high, "core", 1), m
        )

    def wide_piece(pieces, *others):
        pieces = exchange(pieces, "z")
        return wide_sum([after(pieces[0], *others)] + pieces[1:], m)

    def wide_all(wide, *others):
        pairs = [(wide[0], wide[3]), (wide[2], wide[1])]
        pairs = [after(jnp.concatenate(p), *others) for p in pairs]
        return wide + [permute(p, "core", 1) for p in pairs]

    def halfway(parts, *others):
        return middle_sum([after(parts[0], *others)] + parts[1:], m)

    def finished(parts):
        return last_sum(exchange_two(parts, "yx"), m)

    line_a = lined(0)
    line_b = lined(1, line_a)
    basis_a, basis_b = gathered(line_a), gathered(line_b)
    halves_a = first(basis_a, True)
    pieces_a = summed(*halves_a)
    halves_b = first(basis_b, False, pieces_a[0])
    piece_a = wide_piece(pieces_a, halves_b[0])
    wide_a = spread(piece_a, "z")
    pieces_b = summed(*halves_b, wide_a[3])
    parts_a = second(wide_all(wide_a), pieces_b[0])
    wide_b = spread(wide_piece(pieces_b, parts_a[0]), "z")
    parts_a = exchange_two(parts_a, "xy")
    parts_b = second(wide_all(wide_b, parts_a[1], parts_a[2]))
    parts_b = exchange_two(parts_b, "xy")
    blocks_a = halfway(parts_a, parts_b[0])
    blocks_b = halfway(parts_b, blocks_a[0])
    blocks_a = [after(p, parts_b[1], parts_b[2]) for p in blocks_a]
    image = jnp.concatenate([finished(blocks_a), finished(blocks_b)], axis=0)

    core = core.astype(jnp.int32).reshape(1)
    keep, send = local_gram(core, image)
    gram = keep + permute(send, "core", 1)
    for axes in ("zx", "xy", "yz"):
        own, up, down, over = [gram] + [permute_two(gram, axes, hop) for hop in HOPS]
        gram = own + over + (up + down)
    triangle, new_basis = factor(core, gram, permute(gram, "core", 1), image)
    return new_basis, triangle


def solution(mesh):
    in_specs = (
        P("row", "col", None, None, None),
        P("row", "col", None),
        P("row", "col", None),
        P(("row", "col"), None),
    )
    out_specs = (P(("row", "col"), None), P())
    return jax.shard_map(
        per_device, mesh=mesh, in_specs=in_specs, out_specs=out_specs, check_vma=False
    )
```
